256 devices in a mesh: outer: 4 (over z_hi), dev: 64 (over x, z_lo, y, core).
Axes of the slice: x: 4, y: 4, z: 8 (z_hi: 4, z_lo: 2; z = z_hi * 2 + z_lo), core: 2. Of those that a mesh axis runs over, the one named last changes fastest.
Arguments:
- hidden_rows: bfloat16 [65536, 768], P(('outer', 'dev')), may hold values from -6 to 6
- out_grad: bfloat16 [65536, 4096], P(('outer', 'dev')), may hold values from -6 to 6
- expert_weights: bfloat16 [64, 768, 4096], P(None, 'dev', 'outer'), may hold values from -0.21875 to 0.21875
- need_lists: int32 [256, 2], replicated, may hold values from 0 to 63, all different within a row; in each aligned block of 256 rows (0 to 255, 256 to 511, ...) at most 32 rows name the same one
- block_pick: int32 [512], P(('outer', 'dev')), may hold values from 0 to 1
- owner_slot: int32 [64], replicated, may hold values from 0 to 63, each once
Outputs:
- layer_out: bfloat16 [65536, 4096], P(('outer', 'dev'))
- hidden_grad: bfloat16 [65536, 768], P(('outer', 'dev'))
- weight_grad: bfloat16 [64, 768, 4096], P(None, 'dev', 'outer')
The draws below stay inside these ranges and needn't reach their ends.
Inputs may be any that keep to these rules, and one draw needn't show every extreme that they name: `need_lists`: each row names 2 different experts; every expert is named by some row, none by more than 32 rows, a bound that some block reaches.
All inputs are finite; a program needn't handle non-finite values.
Results may differ from the reference program's by a relative error of at most 0.0049.
Values may be sent and summed in bfloat16 or wider, within the bound.
A program may use at most 192 MiB of HBM per device.

```python
import math
import jax
import jax.numpy as jnp
import numpy as np
from jax import lax

D = 4096
FF = 768
NEED = 2
BLOCK = 128
TOK_DEV = 256
E = 64
BLK_DEV = 2
TOKENS = 65536
MOST = 32
DEVICES = 256


def set_ends(values, key, least, high):
    shape = values.shape
    index_at = [jax.random.randint(jax.random.fold_in(key, axis), (), 0, shape[axis]) for axis in range(len(shape))]
    values = values.at[tuple(index_at)].set(least)
    longest = shape.index(max(shape))
    index_at[longest] = (index_at[longest] + 1) % shape[longest]
    return values.at[tuple(index_at)].set(high)


def shard_levels(stream_key, dims, cuts, smallest, top_value):
    factor_of = 1.0
    for axis_at, blocks in cuts:
        heights = jax.random.uniform(jax.random.fold_in(jax.random.fold_in(stream_key, 6), axis_at), (blocks,), jnp.float32, smallest / len(cuts), top_value / len(cuts))
        factor_of = factor_of * jnp.repeat(jnp.exp(heights), dims[axis_at] // blocks).reshape((-1,) + (1,) * (len(dims) - 1 - axis_at))
    return factor_of


def deal_out(key, own, number, rows, number_of, top, bound, lean):
    sequence = jax.random.permutation(key, number_of)
    heavy_load, usual = portions_of(number_of, rows * top, bound, lean, True), portions_of(number_of, rows * top, bound, lean, False)
    places = jnp.arange(number_of)

    def named(sizes, turn):
        used = int((sizes > 0).sum())
        fixed = max(1, used // 4)
        moved = fixed + (places - fixed + turn * (used - fixed)) % max(1, number_of - fixed)
        return jnp.zeros((number_of,), jnp.int32).at[sequence[jnp.where(places < fixed, places, moved)]].set(jnp.asarray(sizes, jnp.int32))

    sizes = jnp.where(number % 4 == 0, named(heavy_load, number // 4), named(usual, number - number // 4 - 1))
    mixed = jax.random.permutation(jax.random.fold_in(own, 3), number_of)
    giver, sink = mixed[0:number_of // 2 * 2:2], mixed[1:number_of // 2 * 2:2]
    slack = jnp.minimum(sizes[giver] - 1, bound - sizes[sink]) // 2
    slack = jnp.where((giver == sequence[0]) | (sink == sequence[0]) | (sizes[sink] == 0), 0, jnp.maximum(slack, 0))
    moved = jax.random.randint(jax.random.fold_in(own, 4), (number_of // 2,), 0, 1 << 20) % (slack + 1)
    sizes = sizes.at[giver].add(-moved).at[sink].add(moved)
    labels = jnp.searchsorted(jnp.cumsum(sizes), jnp.arange(rows * top), side="right").astype(jnp.int32)
    grid = labels.reshape(top, rows).T
    grid = grid[jax.random.permutation(jax.random.fold_in(own, 1), rows)]
    turn = jax.random.randint(jax.random.fold_in(own, 2), (rows, 1), 0, top)
    return jnp.take_along_axis(grid, (jnp.arange(top)[None, :] + turn) % top, axis=1)


def portions_of(count, total, bound, skew, full):
    loads = [(1 << 20) // math.isqrt(standing ** skew) + 1 for standing in range(1, count + 1)]
    largest = bound if full else min(bound, max(-(-total // count), total * loads[0] // sum(loads)))
    least = 1 if total - largest >= count - 1 else 0
    counts, spare = [largest] + [least] * (count - 1), total - largest - least * (count - 1)
    while spare > 0:
        free = [i for i in range(1, count) if counts[i] < largest] or [i for i in range(1, count) if counts[i] < bound]
        mass, budget = sum([loads[i] for i in free]), spare
        for i in free:
            addition = min(bound - counts[i], max(1, budget * loads[i] // mass), spare)
            counts[i] = counts[i] + addition
            spare = spare - addition
    return np.array(counts)


def gaussian(key, extent, deviation, reach, split=(), held_as=jnp.bfloat16):
    entries = deviation * jax.random.normal(key, extent, jnp.float32)
    if split:
        entries = entries * shard_levels(key, extent, split, -0.22, 0.18)
    return jnp.clip(entries, -reach, reach).astype(held_as)


def setup_inputs(seed: int = 0) -> dict:
    key_of = jax.random.split(jax.random.key(seed), 7)
    hidden_rows = gaussian(key_of[0], (TOKENS, FF), 1.0, 6.0, ((0, 256),))
    out_grad = gaussian(key_of[1], (TOKENS, D), 1.0, 6.0, ((0, 256),))
    expert_weights = gaussian(key_of[2], (E, FF, D), FF ** -0.5, 0.21875, ((1, 64), (2, 4)))
    need_lists_keys = jax.random.split(jax.random.fold_in(key_of[3], 1), DEVICES // DEVICES)
    need_lists_turns = jax.random.permutation(jax.random.fold_in(key_of[3], 3), DEVICES // DEVICES)
    need_lists = jax.vmap(lambda own, number: deal_out(jax.random.fold_in(key_of[3], 2), own, number, DEVICES, E, NEED, MOST, 2))(need_lists_keys, need_lists_turns).reshape((DEVICES, NEED))
    block_pick = set_ends(jax.random.randint(key_of[4], (TOKENS // BLOCK,), 0, NEED), jax.random.fold_in(key_of[4], 1), 0, NEED - 1).astype(jnp.int32)
    owner_slot = jax.random.permutation(key_of[5], E).astype(jnp.int32)
    return dict(hidden_rows=hidden_rows, out_grad=out_grad, expert_weights=expert_weights, need_lists=need_lists, block_pick=block_pick, owner_slot=owner_slot)


def reference(hidden_rows, out_grad, expert_weights, need_lists, block_pick, owner_slot):
    slot_table = owner_slot[need_lists]
    picks = block_pick.reshape(DEVICES, BLK_DEV)
    block_slot = jnp.take_along_axis(slot_table, picks, axis=1).reshape(-1)
    hidden_blocks = hidden_rows.reshape(DEVICES * BLK_DEV, BLOCK, FF)
    grad_blocks = out_grad.reshape(DEVICES * BLK_DEV, BLOCK, D)

    def one_block(items):
        block_hidden, block_grad, slot = items
        weight_now = expert_weights[slot]
        forward = jnp.dot(block_hidden, weight_now, preferred_element_type=jnp.float32).astype(jnp.bfloat16)
        backward = jnp.dot(block_grad, weight_now.T, preferred_element_type=jnp.float32).astype(jnp.bfloat16)
        return forward, backward

    layer_out, hidden_grad = lax.map(one_block, (hidden_blocks, grad_blocks, block_slot))

    def one_device(total, index):
        dev_hidden = lax.dynamic_slice_in_dim(hidden_rows, index * TOK_DEV, TOK_DEV, 0)
        dev_grad = lax.dynamic_slice_in_dim(out_grad, index * TOK_DEV, TOK_DEV, 0)
        dev_pick = jnp.repeat(lax.dynamic_index_in_dim(picks, index, 0, keepdims=False), BLOCK, total_repeat_length=TOK_DEV)
        chosen = dev_pick[None, :] == jnp.arange(NEED, dtype=jnp.int32)[:, None]
        masked = jnp.where(chosen[:, :, None], dev_hidden[None].astype(jnp.float32), jnp.float32(0.0))
        partial_value = jnp.einsum("kts,td->ksd", masked, dev_grad.astype(jnp.float32)).astype(jnp.bfloat16)
        slots_now = lax.dynamic_index_in_dim(slot_table, index, 0, keepdims=False)
        total = total.at[slots_now].add(partial_value.astype(jnp.float32))
        return total, None

    start = jnp.zeros((E, FF, D), jnp.float32)
    summed, unused = lax.scan(one_device, start, jnp.arange(DEVICES, dtype=jnp.int32))
    return layer_out.reshape(TOKENS, D), hidden_grad.reshape(TOKENS, FF), summed.astype(jnp.bfloat16)
```

```python
import functools

import jax
import jax.numpy as jnp
from jax import lax
from jax.experimental import pallas as pl
from jax.experimental.pallas import tpu as pltpu
from jax.sharding import PartitionSpec as P

MESH = pl.DeviceIdType.MESH
BLOCK = 128
NX, NY, NZ, NC = 4, 4, 8, 2
ROWS = 12
GROUP = 192
COLS = 256
TOK = 256
EXPERTS = 64
VMEM_LIMIT = 60 * 2**20
OFFSETS = [(dz, dc) for dz in (0, 1, -1, 2, -2, 3, -3, 4) for dc in (0, 1)]


def coords():
    o, d = lax.axis_index("outer"), lax.axis_index("dev")
    return d // 16, (d // 2) % 4, o * 2 + (d // 8) % 2, d % 2


def device(x, y, z, c):
    return (z // 2, x * 16 + (z % 2) * 8 + y * 2 + c)


class Copies:
    def __init__(self, send, recv):
        self.send, self.recv, self.used, self.pending = send, recv, 0, []

    def start(self, src, dst, target, land):
        n = self.used
        self.used += 1
        copy = pltpu.make_async_remote_copy(src, dst, self.send.at[n], self.recv.at[n], device_id=target, device_id_type=MESH)
        copy.start()
        self.pending.append(copy)
        back = pltpu.make_async_remote_copy(land, land, self.send.at[n], self.recv.at[n], device_id=target, device_id_type=MESH)
        return back

    def local(self, src, dst):
        n = self.used
        self.used += 1
        copy = pltpu.make_async_copy(src, dst, self.recv.at[n])
        copy.start()
        return copy

    def drain(self):
        for copy in self.pending:
            copy.wait_send()


def greet(x, y, z, c):
    barrier = pltpu.get_barrier_semaphore()
    others = [(x, y, (z + dz + NZ) % NZ, (c + dc) % 2) for dz, dc in OFFSETS[1:]]
    others += [(x, (y + dy) % NY, z, c) for dy in (1, 2, 3)]
    others += [((x + dx) % NX, y, z, c) for dx in (1, 3)]
    for other in others:
        pl.semaphore_signal(barrier, inc=1, device_id=device(*other), device_id_type=MESH)
    pl.semaphore_wait(barrier, len(others))


def quarter(q):
    return pl.ds(pl.multiple_of(q * COLS, COLS), COLS)


def gather_kernel(w, h, g, wg, hg, gg, send, recv):
    x, y, z, c = coords()
    greet(x, y, z, c)
    cp = Copies(send, recv)
    zof = lambda d: (z + d + NZ) % NZ
    yof = lambda d: (y + d + NY) % NY
    xof = lambda d: (x + d + NX) % NX
    zl = z % 2
    here = zl * 2 + c

    w1 = []
    for dl, dc in ((0, 1), (1, 0), (1, 1)):
        ol, oc = (zl + dl) % 2, (c + dc) % 2
        there = ol * 2 + oc
        w1.append(cp.start(w.at[:, :, quarter(there)], wg.at[x, here], device(x, y, (z // 2) * 2 + ol, oc), wg.at[x, there]))
    w1.append(cp.local(w.at[:, :, quarter(here)], wg.at[x, here]))
    h1 = []
    for dy in (1, 3, 2):
        oy = yof(dy)
        h1.append(cp.start(h.at[oy], hg.at[z, c, y], device(x, oy, z, c), hg.at[z, c, yof(-dy)]))
    h1.append(cp.local(h.at[y], hg.at[z, c, y]))
    g1 = []
    for dz, dc in OFFSETS:
        if (dz, dc) == (0, 0):
            g1.append(cp.local(g.at[:, quarter(z * 2 + c)], gg.at[z, c, y]))
            continue
        oz, oc = zof(dz), (c + dc) % 2
        g1.append(cp.start(g.at[:, quarter(oz * 2 + oc)], gg.at[z, c, y], device(x, y, oz, oc), gg.at[zof(-dz), oc, y]))

    def wait(copy):
        if hasattr(copy, "wait_recv") and copy.is_remote:
            copy.wait_recv()
        else:
            copy.wait()

    up_z, down_z = device(x, y, zof(1), c), device(x, y, zof(-1), c)
    up_y, down_y = device(x, yof(1), z, c), device(x, yof(-1), z, c)
    up_x, down_x = device(xof(1), y, z, c), device(xof(-1), y, z, c)
    sibling = device(x, y, z, (c + 1) % 2)

    h_state = {}
    h_sib = []

    def h_step(s):
        if s == 0:
            for copy in h1:
                wait(copy)
        else:
            wait(h_state["up"])
            wait(h_state["down"])
        behind, ahead = zof(-s), zof(s)
        if s < 3:
            h_state["up"] = cp.start(hg.at[behind, c], hg.at[behind, c], up_z, hg.at[zof(-s - 1), c])
            h_state["down"] = cp.start(hg.at[ahead, c], hg.at[ahead, c], down_z, hg.at[zof(s + 1), c])
        elif s == 3:
            h_state["up"] = cp.start(hg.at[behind, c, 0:2], hg.at[behind, c, 0:2], up_z, hg.at[zof(-4), c, 0:2])
            h_state["down"] = cp.start(hg.at[ahead, c, 2:4], hg.at[ahead, c, 2:4], down_z, hg.at[zof(4), c, 2:4])
        for zz in [behind] if s in (0, 4) else [behind, ahead]:
            h_sib.append(cp.start(hg.at[zz, c], hg.at[zz, c], sibling, hg.at[zz, (c + 1) % 2]))

    w_state = {}

    def w_step(s):
        if s == 0:
            for copy in w1:
                wait(copy)
            w_state["up"] = cp.start(wg.at[x], wg.at[x], up_x, wg.at[xof(-1)])
            w_state["down"] = cp.start(wg.at[x], wg.at[x], down_x, wg.at[xof(1)])
        else:
            wait(w_state["up"])
            wait(w_state["down"])
            if s == 1:
                w_state["up"] = cp.start(wg.at[xof(-1), 0:2], wg.at[xof(-1), 0:2], up_x, wg.at[xof(-2), 0:2])
                w_state["down"] = cp.start(wg.at[xof(1), 2:4], wg.at[xof(1), 2:4], down_x, wg.at[xof(2), 2:4])

    g2, g3 = [], []
    half = TOK // 2

    def g_first(k):
        wait(g1[k])
        dz, dc = OFFSETS[k]
        zs, cs = zof(-dz), (c + dc) % 2
        mine = gg.at[zs, cs, y]
        g2.append((cp.start(mine, mine, up_y, gg.at[zs, cs, yof(-1)]), cp.start(mine, mine, down_y, gg.at[zs, cs, yof(1)])))

    def g_second(k):
        dz, dc = OFFSETS[k]
        zs, cs = zof(-dz), (c + dc) % 2
        for copy in g2[k]:
            wait(copy)
        below = gg.at[zs, cs, yof(-1), 0:half]
        above = gg.at[zs, cs, yof(1), half:TOK]
        g3.append(cp.start(below, below, up_y, gg.at[zs, cs, yof(-2), 0:half]))
        g3.append(cp.start(above, above, down_y, gg.at[zs, cs, yof(2), half:TOK]))

    g_first(0)
    h_step(0)
    w_step(0)
    steps = len(OFFSETS)
    for k in range(1, steps):
        g_first(k)
        if k >= 2:
            g_second(k - 2)
        if k in (4, 7, 10, 13):
            h_step((k - 1) // 3)
        if k == 8:
            w_step(1)
    g_second(steps - 2)
    g_second(steps - 1)
    w_step(2)
    for copy in g3 + h_sib:
        wait(copy)
    cp.drain()


def compute_kernel(slots, w, h, g, lo, hgrad, dw, wf, acc):
    step = pl.program_id(0)
    lanes = [slice(j * 128, (j + 1) * 128) for j in range(COLS // 128)]

    @pl.when(step == 0)
    def _():
        def fill(i, carry):
            rows = pl.ds(pl.multiple_of(i * 256, 256), 256)
            for j, lane in enumerate(lanes):
                wf[j, rows, :] = w[rows, lane].astype(jnp.float32)
                acc[j, rows, :] = jnp.zeros((256, 128), jnp.float32)
            return carry

        lax.fori_loop(0, GROUP * EXPERTS // 256, fill, 0)

    for b in range(TOK // BLOCK):
        slot = slots[step * (TOK // BLOCK) + b]
        rows = pl.ds(slot, GROUP, stride=EXPERTS)
        weight = jnp.concatenate([wf[j, rows, :] for j in range(len(lanes))], axis=1).astype(jnp.bfloat16)
        tokens = slice(b * BLOCK, (b + 1) * BLOCK)
        hid = h[0, :, tokens]
        cot = g[0, tokens, :]
        lo[0, tokens, :] = lax.dot_general(
            hid, weight, (((0,), (0,)), ((), ())), preferred_element_type=jnp.float32
        ).astype(jnp.bfloat16)
        hgrad[0, :, tokens] = lax.dot_general(
            weight, cot, (((1,), (1,)), ((), ())), preferred_element_type=jnp.float32
        ).astype(jnp.bfloat16)
        outer = jnp.dot(hid, cot, preferred_element_type=jnp.float32)
        for j, lane in enumerate(lanes):
            acc[j, rows, :] += outer[:, lane]

    @pl.when(step == pl.num_programs(0) - 1)
    def _():
        def empty(i, carry):
            rows = pl.ds(pl.multiple_of(i * 256, 256), 256)
            for j, lane in enumerate(lanes):
                dw[rows, lane] = acc[j, rows, :].astype(jnp.bfloat16)
            return carry

        lax.fori_loop(0, GROUP * EXPERTS // 256, empty, 0)


def add_into(dst, *others):
    lead = dst.shape[:-2]
    rows = dst.shape[-2]
    cut = 64
    per = rows // cut
    total = per
    for n in lead:
        total *= n

    def one(i, carry):
        where, rest = [], i // per
        for n in reversed(lead):
            where.insert(0, rest % n)
            rest = rest // n
        at = tuple(where) + (pl.ds(pl.multiple_of((i % per) * cut, cut), cut), slice(None))
        value = dst[at].astype(jnp.float32)
        for other in others:
            value += other[at].astype(jnp.float32)
        dst[at] = value.astype(jnp.bfloat16)
        return carry

    lax.fori_loop(0, total, one, 0)


def scatter_kernel(lo, hp, dw, out, hout, wout, lo_half_up, lo_half_dn, lo_up, lo_dn, sib, hp_up, hp_dn, dw_half_up, dw_half_dn, dw_up, dw_dn, send, recv):
    x, y, z, c = coords()
    greet(x, y, z, c)
    cp = Copies(send, recv)
    zof = lambda d: (z + d + NZ) % NZ
    yof = lambda d: (y + d + NY) % NY
    xof = lambda d: (x + d + NX) % NX
    zl = z % 2
    here = zl * 2 + c
    up_z, down_z = device(x, y, zof(1), c), device(x, y, zof(-1), c)
    up_y, down_y = device(x, yof(1), z, c), device(x, yof(-1), z, c)
    up_x, down_x = device(xof(1), y, z, c), device(xof(-1), y, z, c)
    sibling = device(x, y, z, (c + 1) % 2)
    half = TOK // 2
    order = list(reversed(OFFSETS))

    sib_in = {}
    for d in (4, 3, -3, 2, -2, 1, -1, 0):
        zz = zof(d)
        sib_in[d] = cp.start(hp.at[zz, (c + 1) % 2], sib.at[zz], sibling, sib.at[zz])
    a_in = []
    for k, (dz, dc) in enumerate(order):
        zs, cs = zof(dz), (c + dc) % 2
        a_in.append((
            cp.start(lo.at[zs, cs, yof(2), 0:half], lo_half_up.at[k], up_y, lo_half_up.at[k]),
            cp.start(lo.at[zs, cs, yof(2), half:TOK], lo_half_dn.at[k], down_y, lo_half_dn.at[k]),
        ))
    d_in = (
        cp.start(dw.at[xof(2), 0:2], dw_half_up, up_x, dw_half_up),
        cp.start(dw.at[xof(2), 2:4], dw_half_dn, down_x, dw_half_dn),
    )

    h_state = {}

    def h_step(s):
        for d in (4,) if s == 4 else (s, -s) if s else (0,):
            sib_in[d].wait_recv()
        if s < 4:
            h_state["up"].wait_recv()
            h_state["down"].wait_recv()
        if s == 4:
            add_into(hp.at[zof(4), c], sib.at[zof(4)])
            h_state["up"] = cp.start(hp.at[zof(4), c, 0:2], hp_up.at[3, 0:2], up_z, hp_up.at[3, 0:2])
            h_state["down"] = cp.start(hp.at[zof(4), c, 2:4], hp_dn.at[3, 2:4], down_z, hp_dn.at[3, 2:4])
            return
        if s == 3:
            add_into(hp.at[zof(3), c, 0:2], sib.at[zof(3), 0:2], hp_up.at[3, 0:2])
            add_into(hp.at[zof(3), c, 2:4], sib.at[zof(3), 2:4])
            add_into(hp.at[zof(-3), c, 0:2], sib.at[zof(-3), 0:2])
            add_into(hp.at[zof(-3), c, 2:4], sib.at[zof(-3), 2:4], hp_dn.at[3, 2:4])
        elif s > 0:
            add_into(hp.at[zof(s), c], sib.at[zof(s)], hp_up.at[s])
            add_into(hp.at[zof(-s), c], sib.at[zof(-s)], hp_dn.at[s])
        else:
            add_into(hp.at[z, c], sib.at[z], hp_up.at[0], hp_dn.at[0])
        if s > 0:
            h_state["up"] = cp.start(hp.at[zof(s), c], hp_up.at[s - 1], up_z, hp_up.at[s - 1])
            h_state["down"] = cp.start(hp.at[zof(-s), c], hp_dn.at[s - 1], down_z, hp_dn.at[s - 1])

    b_in, o_in = [], []

    def lo_second(k):
        dz, dc = order[k]
        zs, cs = zof(dz), (c + dc) % 2
        a_in[k][0].wait_recv()
        add_into(lo.at[zs, cs, yof(1), 0:half], lo_half_up.at[k])
        first = cp.start(lo.at[zs, cs, yof(1)], lo_up.at[k], up_y, lo_up.at[k])
        a_in[k][1].wait_recv()
        add_into(lo.at[zs, cs, yof(-1), half:TOK], lo_half_dn.at[k])
        b_in.append((first, cp.start(lo.at[zs, cs, yof(-1)], lo_dn.at[k], down_y, lo_dn.at[k])))

    def lo_third(k):
        dz, dc = order[k]
        zs, cs = zof(dz), (c + dc) % 2
        for copy in b_in[k]:
            copy.wait_recv()
        add_into(lo.at[zs, cs, y], lo_up.at[k], lo_dn.at[k])
        mine = out.at[:, quarter(z * 2 + c)]
        if (dz, dc) == (0, 0):
            o_in.append(cp.local(lo.at[zs, cs, y], mine))
        else:
            o_in.append(cp.start(lo.at[zs, cs, y], mine, device(x, y, zs, cs), out.at[:, quarter(zof(-dz) * 2 + cs)]))

    d_state = {}

    def d_step(s):
        if s == 0:
            d_in[0].wait_recv()
            add_into(dw.at[xof(1), 0:2], dw_half_up)
            d_state["up"] = cp.start(dw.at[xof(1)], dw_up, up_x, dw_up)
            d_in[1].wait_recv()
            add_into(dw.at[xof(-1), 2:4], dw_half_dn)
            d_state["down"] = cp.start(dw.at[xof(-1)], dw_dn, down_x, dw_dn)
            return
        d_state["up"].wait_recv()
        d_state["down"].wait_recv()
        add_into(dw.at[x], dw_up, dw_dn)
        for dl, dc in ((1, 0), (1, 1), (0, 1)):
            ol, oc = (zl + dl) % 2, (c + dc) % 2
            there = ol * 2 + oc
            o_in.append(cp.start(dw.at[x, there], wout.at[:, :, quarter(here)], device(x, y, (z // 2) * 2 + ol, oc), wout.at[:, :, quarter(there)]))
        o_in.append(cp.local(dw.at[x, here], wout.at[:, :, quarter(here)]))

    h_step(4)
    steps = len(order)
    for k in range(steps):
        lo_second(k)
        if k >= 2:
            lo_third(k - 2)
        if k in (3, 6, 9, 12):
            h_step(4 - k // 3)
        if k == 4:
            d_step(0)
        if k == 10:
            d_step(1)
    for dy in (1, 3, 2):
        oy = yof(dy)
        o_in.append(cp.start(hp.at[z, c, oy], hout.at[y], device(x, oy, z, c), hout.at[yof(-dy)]))
    o_in.append(cp.local(hp.at[z, c, y], hout.at[y]))
    lo_third(steps - 2)
    lo_third(steps - 1)
    for copy in o_in:
        if copy.is_remote:
            copy.wait_recv()
        else:
            copy.wait()
    cp.drain()


def body(hidden_rows, out_grad, expert_weights, need_lists, block_pick, owner_slot):
    bf16 = jnp.bfloat16
    shape = jax.ShapeDtypeStruct
    anywhere = pl.BlockSpec(memory_space=pl.ANY)
    vmem = pl.BlockSpec(memory_space=pltpu.VMEM)
    x = lax.axis_index("dev") // 16

    picks = lax.all_gather(block_pick, ("outer", "dev"), axis=0, tiled=True).reshape(256, 2)
    experts = jnp.where(picks == 0, need_lists[:, 0:1], need_lists[:, 1:2])
    ids = jnp.arange(EXPERTS, dtype=jnp.int32)
    slots = jnp.sum(jnp.where(experts[:, :, None] == ids, owner_slot[None, None, :], 0), axis=2)
    slots = slots.reshape(4, NX, 2, NY, NC, 2)
    slots = lax.dynamic_index_in_dim(slots, x, 1, keepdims=False).transpose(0, 1, 3, 2, 4).reshape(-1)

    ht = hidden_rows.reshape(TOK, NX, 2, NY, NC, ROWS).transpose(3, 1, 2, 4, 5, 0).reshape(NY, GROUP, TOK)
    wt = expert_weights.transpose(1, 0, 2)

    wg, hg, gg = pl.pallas_call(
        gather_kernel,
        out_shape=(
            shape((NX, 4, ROWS, EXPERTS, COLS), bf16),
            shape((NZ, NC, NY, GROUP, TOK), bf16),
            shape((NZ, NC, NY, TOK, COLS), bf16),
        ),
        in_specs=[anywhere] * 3,
        out_specs=(anywhere,) * 3,
        scratch_shapes=[pltpu.SemaphoreType.DMA((128,)), pltpu.SemaphoreType.DMA((128,))],
        compiler_params=pltpu.CompilerParams(collective_id=0, has_side_effects=True, vmem_limit_bytes=VMEM_LIMIT),
        name="gather",
    )(wt, ht, out_grad)

    sources = NZ * NC * NY
    one = lambda rows: pl.BlockSpec((1, rows, 256), lambda i, s: (i, 0, 0))
    whole = lambda: pl.BlockSpec((GROUP * EXPERTS, COLS), lambda i, s: (0, 0), pipeline_mode=pl.Buffered(1))
    lo, hp, dw = pl.pallas_call(
        compute_kernel,
        grid_spec=pltpu.PrefetchScalarGridSpec(
            num_scalar_prefetch=1,
            grid=(sources,),
            in_specs=[whole(), one(GROUP), one(TOK)],
            out_specs=(one(TOK), one(GROUP), whole()),
            scratch_shapes=[
                pltpu.VMEM((COLS // 128, GROUP * EXPERTS, 128), jnp.float32),
                pltpu.VMEM((COLS // 128, GROUP * EXPERTS, 128), jnp.float32),
            ],
        ),
        out_shape=(
            shape((sources, TOK, COLS), bf16),
            shape((sources, GROUP, TOK), bf16),
            shape((GROUP * EXPERTS, COLS), bf16),
        ),
        compiler_params=pltpu.CompilerParams(vmem_limit_bytes=VMEM_LIMIT),
        name="compute",
    )(slots, wg.reshape(GROUP * EXPERTS, COLS), hg.reshape(sources, GROUP, TOK), gg.reshape(sources, TOK, COLS))

    half = TOK // 2
    pieces = len(OFFSETS)
    layer_out, hidden, weight_grad = pl.pallas_call(
        scatter_kernel,
        out_shape=(
            shape((TOK, 4096), bf16),
            shape((NY, GROUP, TOK), bf16),
            shape((ROWS, EXPERTS, 1024), bf16),
        ),
        in_specs=[vmem] * 3,
        out_specs=(anywhere,) * 3,
        scratch_shapes=[
            pltpu.VMEM((pieces, half, COLS), bf16),
            pltpu.VMEM((pieces, half, COLS), bf16),
            pltpu.VMEM((pieces, TOK, COLS), bf16),
            pltpu.VMEM((pieces, TOK, COLS), bf16),
            pltpu.VMEM((NZ, NY, GROUP, TOK), bf16),
            pltpu.VMEM((4, NY, GROUP, TOK), bf16),
            pltpu.VMEM((4, NY, GROUP, TOK), bf16),
            pltpu.VMEM((2, ROWS, EXPERTS, COLS), bf16),
            pltpu.VMEM((2, ROWS, EXPERTS, COLS), bf16),
            pltpu.VMEM((4, ROWS, EXPERTS, COLS), bf16),
            pltpu.VMEM((4, ROWS, EXPERTS, COLS), bf16),
            pltpu.SemaphoreType.DMA((128,)),
            pltpu.SemaphoreType.DMA((128,)),
        ],
        compiler_params=pltpu.CompilerParams(collective_id=1, has_side_effects=True, vmem_limit_bytes=VMEM_LIMIT),
        name="scatter",
    )(
        lo.reshape(NZ, NC, NY, TOK, COLS),
        hp.reshape(NZ, NC, NY, GROUP, TOK),
        dw.reshape(NX, 4, ROWS, EXPERTS, COLS),
    )
    hidden_grad = hidden.reshape(NY, NX, 2, NC, ROWS, TOK).transpose(5, 1, 2, 0, 3, 4).reshape(TOK, -1)
    return layer_out, hidden_grad, weight_grad.transpose(1, 0, 2)


def solution(mesh):
    return jax.shard_map(
        body,
        mesh=mesh,
        in_specs=(
            P(("outer", "dev"), None),
            P(("outer", "dev"), None),
            P(None, "dev", "outer"),
            P(),
            P(("outer", "dev")),
            P(),
        ),
        out_specs=(P(("outer", "dev"), None), P(("outer", "dev"), None), P(None, "dev", "outer")),
        check_vma=False,
    )
```

```python
import functools

import jax
import jax.numpy as jnp
from jax import lax
from jax.experimental import pallas as pl
from jax.experimental.pallas import tpu as pltpu
from jax.sharding import PartitionSpec as P

MESH = pl.DeviceIdType.MESH
BLOCK = 128
NX, NY, NZ, NC = 4, 4, 8, 2
ROWS = 12
GROUP = 192
COLS = 256
TOK = 256
EXPERTS = 64
VMEM_LIMIT = 60 * 2**20
OFFSETS = [(dz, dc) for dz in (0, 1, -1, 2, -2, 3, -3, 4) for dc in (0, 1)]


def coords():
    o, d = lax.axis_index("outer"), lax.axis_index("dev")
    return d // 16, (d // 2) % 4, o * 2 + (d // 8) % 2, d % 2


def device(x, y, z, c):
    return (z // 2, x * 16 + (z % 2) * 8 + y * 2 + c)


class Copies:
    def __init__(self, send, recv):
        self.send, self.recv, self.used, self.pending = send, recv, 0, []

    def start(self, src, dst, target, land):
        n = self.used
        self.used += 1
        copy = pltpu.make_async_remote_copy(src, dst, self.send.at[n], self.recv.at[n], device_id=target, device_id_type=MESH)
        copy.start()
        self.pending.append(copy)
        back = pltpu.make_async_remote_copy(land, land, self.send.at[n], self.recv.at[n], device_id=target, device_id_type=MESH)
        return back

    def local(self, src, dst):
        n = self.used
        self.used += 1
        copy = pltpu.make_async_copy(src, dst, self.recv.at[n])
        copy.start()
        return copy

    def drain(self):
        for copy in self.pending:
            copy.wait_send()


def greet(x, y, z, c):
    barrier = pltpu.get_barrier_semaphore()
    others = [(x, y, (z + dz + NZ) % NZ, (c + dc) % 2) for dz, dc in OFFSETS[1:]]
    others += [(x, (y + dy) % NY, z, c) for dy in (1, 2, 3)]
    others += [((x + dx) % NX, y, z, c) for dx in (1, 3)]
    for other in others:
        pl.semaphore_signal(barrier, inc=1, device_id=device(*other), device_id_type=MESH)
    pl.semaphore_wait(barrier, len(others))


def quarter(q):
    return pl.ds(pl.multiple_of(q * COLS, COLS), COLS)


def gather_kernel(w, h, g, pick, wg, hg, gg, picks, landed, wide, turned, send, recv):
    x, y, z, c = coords()
    greet(x, y, z, c)
    cp = Copies(send, recv)
    zof = lambda d: (z + d + NZ) % NZ
    yof = lambda d: (y + d + NY) % NY
    xof = lambda d: (x + d + NX) % NX
    zl = z % 2
    here = zl * 2 + c

    h1 = []
    for dy in (1, 3, 2):
        oy = yof(dy)
        h1.append(cp.start(h.at[oy], hg.at[z, c, y], device(x, oy, z, c), hg.at[z, c, yof(-dy)]))
        h1.append(cp.start(pick, picks.at[z, c, y], device(x, oy, z, c), picks.at[z, c, yof(-dy)]))
    h1.append(cp.local(h.at[y], hg.at[z, c, y]))
    h1.append(cp.local(pick, picks.at[z, c, y]))
    w1 = []
    for dl, dc in ((1, 0), (1, 1), (0, 1)):
        ol, oc = (zl + dl) % 2, (c + dc) % 2
        there = ol * 2 + oc
        w1.append(cp.start(w.at[:, :, quarter(there)], landed.at[here], device(x, y, (z // 2) * 2 + ol, oc), landed.at[there]))
    w1.append(cp.local(w.at[:, :, quarter(here)], landed.at[here]))

    g1 = []

    def g_start(k):
        dz, dc = OFFSETS[k]
        if (dz, dc) == (0, 0):
            g1.append(cp.local(g.at[:, quarter(z * 2 + c)], gg.at[z, c, y]))
            return
        oz, oc = zof(dz), (c + dc) % 2
        g1.append(cp.start(g.at[:, quarter(oz * 2 + oc)], gg.at[z, c, y], device(x, y, oz, oc), gg.at[zof(-dz), oc, y]))

    def wait(copy):
        if copy.is_remote:
            copy.wait_recv()
        else:
            copy.wait()

    up_z, down_z = device(x, y, zof(1), c), device(x, y, zof(-1), c)
    up_y, down_y = device(x, yof(1), z, c), device(x, yof(-1), z, c)
    up_x, down_x = device(xof(1), y, z, c), device(xof(-1), y, z, c)
    sibling = device(x, y, z, (c + 1) % 2)

    h_state = []
    h_sib = []

    def h_send(pairs, target, back):
        for ref, at, land in pairs:
            back.append(cp.start(ref.at[at], ref.at[at], target, ref.at[land]))

    def h_step(s):
        for copy in h1 if s == 0 else list(h_state):
            wait(copy)
        h_state.clear()
        behind, ahead = zof(-s), zof(s)
        if s < 3:
            h_send([(hg, (behind, c), (zof(-s - 1), c)), (picks, (behind, c), (zof(-s - 1), c))], up_z, h_state)
            h_send([(hg, (ahead, c), (zof(s + 1), c)), (picks, (ahead, c), (zof(s + 1), c))], down_z, h_state)
        elif s == 3:
            low, high = slice(0, 2), slice(2, 4)
            h_send([(hg, (behind, c, low), (zof(-4), c, low)), (picks, (behind, c, low), (zof(-4), c, low))], up_z, h_state)
            h_send([(hg, (ahead, c, high), (zof(4), c, high)), (picks, (ahead, c, high), (zof(4), c, high))], down_z, h_state)
        for zz in [behind] if s in (0, 4) else [behind, ahead]:
            h_send([(r, (zz, c), (zz, (c + 1) % 2)) for r in (hg, picks)], sibling, h_sib)

    w_state = {}
    bf16 = jnp.bfloat16
    span = ROWS * 4

    def w_step(s):
        if s == 0:
            for copy in w1:
                wait(copy)

            def widen(i, carry):
                q, r = i // ROWS, i % ROWS
                rows = pl.ds(pl.multiple_of(i * EXPERTS, EXPERTS), EXPERTS)
                for j in range(COLS // 128):
                    wide[j, rows, :] = landed[q, r, :, j * 128 : (j + 1) * 128].astype(jnp.float32)
                return carry

            lax.fori_loop(0, span, widen, 0)

            def turn(e, carry):
                for j in range(COLS // 128):
                    turned[e, :, j * 128 : (j + 1) * 128] = wide[j, pl.ds(e, span, stride=EXPERTS), :].astype(bf16)
                return carry

            lax.fori_loop(0, EXPERTS, turn, 0)
            w_state["up"] = cp.start(turned, wg.at[x], up_x, wg.at[xof(-1)])
            w_state["down"] = cp.start(turned, wg.at[x], down_x, wg.at[xof(1)])
            w_state["own"] = cp.local(turned, wg.at[x])
        else:
            wait(w_state["up"])
            wait(w_state["down"])
            if s == 1:
                low, high = slice(0, EXPERTS // 2), slice(EXPERTS // 2, EXPERTS)
                w_state["up"] = cp.start(wg.at[xof(-1), low], wg.at[xof(-1), low], up_x, wg.at[xof(-2), low])
                w_state["down"] = cp.start(wg.at[xof(1), high], wg.at[xof(1), high], down_x, wg.at[xof(2), high])
            else:
                wait(w_state["own"])

    g2, g3 = [], []
    half = TOK // 2

    def g_first(k):
        wait(g1[k])
        dz, dc = OFFSETS[k]
        zs, cs = zof(-dz), (c + dc) % 2
        mine = gg.at[zs, cs, y]
        g2.append((cp.start(mine, mine, up_y, gg.at[zs, cs, yof(-1)]), cp.start(mine, mine, down_y, gg.at[zs, cs, yof(1)])))

    def g_second(k):
        dz, dc = OFFSETS[k]
        zs, cs = zof(-dz), (c + dc) % 2
        for copy in g2[k]:
            wait(copy)
        below = gg.at[zs, cs, yof(-1), 0:half]
        above = gg.at[zs, cs, yof(1), half:TOK]
        g3.append(cp.start(below, below, up_y, gg.at[zs, cs, yof(-2), 0:half]))
        g3.append(cp.start(above, above, down_y, gg.at[zs, cs, yof(2), half:TOK]))

    steps = len(OFFSETS)
    for k in range(steps):
        g_start(k)
    g_first(0)
    h_step(0)
    g_first(1)
    w_step(0)
    for k in range(2, steps):
        g_first(k)
        g_second(k - 2)
        if k in (4, 7, 10, 13):
            h_step((k - 1) // 3)
        if k == 8:
            w_step(1)
    g_second(steps - 2)
    g_second(steps - 1)
    w_step(2)
    for copy in g3 + h_sib:
        wait(copy)
    cp.drain()


def compute_kernel(slots, w, h, g, lo, hgrad, dw, acc):
    step = pl.program_id(0)
    span = ROWS * 4

    @pl.when(step == 0)
    def _():
        def clear(e, carry):
            for j in range(NX):
                acc[j, e] = jnp.zeros((span, COLS), jnp.float32)
            return carry

        lax.fori_loop(0, EXPERTS, clear, 0)

    for n in range(h.shape[0]):
        for b in range(TOK // BLOCK):
            slot = slots[(step * h.shape[0] + n) * (TOK // BLOCK) + b]
            weight = jnp.concatenate([w[j, slot] for j in range(NX)], axis=0)
            tokens = slice(b * BLOCK, (b + 1) * BLOCK)
            hid = h[n, :, tokens]
            cot = g[n, tokens, :]
            lo[n, tokens, :] = lax.dot_general(
                hid, weight, (((0,), (0,)), ((), ())), preferred_element_type=jnp.float32
            ).astype(jnp.bfloat16)
            hgrad[n, :, tokens] = lax.dot_general(
                weight, cot, (((1,), (1,)), ((), ())), preferred_element_type=jnp.float32
            ).astype(jnp.bfloat16)
            outer = jnp.dot(hid, cot, preferred_element_type=jnp.float32)
            for j in range(NX):
                acc[j, slot] += outer[j * span : (j + 1) * span]

    @pl.when(step == pl.num_programs(0) - 1)
    def _():
        def empty(e, carry):
            for j in range(NX):
                dw[j, e] = acc[j, e].astype(jnp.bfloat16)
            return carry

        lax.fori_loop(0, EXPERTS, empty, 0)


def add_into(dst, *others):
    lead = dst.shape[:-2]
    rows = dst.shape[-2]
    cut = min(rows, 64)
    per = rows // cut
    total = per
    for n in lead:
        total *= n

    def one(i, carry):
        where, rest = [], i // per
        for n in reversed(lead):
            where.insert(0, rest % n)
            rest = rest // n
        at = tuple(where) + (pl.ds(pl.multiple_of((i % per) * cut, cut), cut), slice(None))
        value = dst[at].astype(jnp.float32)
        for other in others:
            value += other[at].astype(jnp.float32)
        dst[at] = value.astype(jnp.bfloat16)
        return carry

    lax.fori_loop(0, total, one, 0)


def scatter_kernel(lo, hp, dw, out, hout, wout, lo_half_up, lo_half_dn, lo_up, lo_dn, sib, hp_up, hp_dn, dw_half_up, dw_half_dn, dw_up, dw_dn, wide, turned, send, recv):
    x, y, z, c = coords()
    greet(x, y, z, c)
    cp = Copies(send, recv)
    zof = lambda d: (z + d + NZ) % NZ
    yof = lambda d: (y + d + NY) % NY
    xof = lambda d: (x + d + NX) % NX
    zl = z % 2
    here = zl * 2 + c
    up_z, down_z = device(x, y, zof(1), c), device(x, y, zof(-1), c)
    up_y, down_y = device(x, yof(1), z, c), device(x, yof(-1), z, c)
    up_x, down_x = device(xof(1), y, z, c), device(xof(-1), y, z, c)
    sibling = device(x, y, z, (c + 1) % 2)
    half = TOK // 2
    order = list(reversed(OFFSETS))

    sib_in = {}
    for d in (4, 3, -3, 2, -2, 1, -1, 0):
        zz = zof(d)
        sib_in[d] = cp.start(hp.at[zz, (c + 1) % 2], sib.at[zz], sibling, sib.at[zz])
    a_in = []
    for k, (dz, dc) in enumerate(order):
        zs, cs = zof(dz), (c + dc) % 2
        a_in.append((
            cp.start(lo.at[zs, cs, yof(2), 0:half], lo_half_up.at[k], up_y, lo_half_up.at[k]),
            cp.start(lo.at[zs, cs, yof(2), half:TOK], lo_half_dn.at[k], down_y, lo_half_dn.at[k]),
        ))
    d_in = (
        cp.start(dw.at[xof(2), 0 : EXPERTS // 2], dw_half_up, up_x, dw_half_up),
        cp.start(dw.at[xof(2), EXPERTS // 2 : EXPERTS], dw_half_dn, down_x, dw_half_dn),
    )

    h_state = {}

    def h_step(s):
        for d in (4,) if s == 4 else (s, -s) if s else (0,):
            sib_in[d].wait_recv()
        if s < 4:
            h_state["up"].wait_recv()
            h_state["down"].wait_recv()
        if s == 4:
            add_into(hp.at[zof(4), c], sib.at[zof(4)])
            h_state["up"] = cp.start(hp.at[zof(4), c, 0:2], hp_up.at[3, 0:2], up_z, hp_up.at[3, 0:2])
            h_state["down"] = cp.start(hp.at[zof(4), c, 2:4], hp_dn.at[3, 2:4], down_z, hp_dn.at[3, 2:4])
            return
        if s == 3:
            add_into(hp.at[zof(3), c, 0:2], sib.at[zof(3), 0:2], hp_up.at[3, 0:2])
            add_into(hp.at[zof(3), c, 2:4], sib.at[zof(3), 2:4])
            add_into(hp.at[zof(-3), c, 0:2], sib.at[zof(-3), 0:2])
            add_into(hp.at[zof(-3), c, 2:4], sib.at[zof(-3), 2:4], hp_dn.at[3, 2:4])
        elif s > 0:
            add_into(hp.at[zof(s), c], sib.at[zof(s)], hp_up.at[s])
            add_into(hp.at[zof(-s), c], sib.at[zof(-s)], hp_dn.at[s])
        else:
            add_into(hp.at[z, c], sib.at[z], hp_up.at[0], hp_dn.at[0])
        if s > 0:
            h_state["up"] = cp.start(hp.at[zof(s), c], hp_up.at[s - 1], up_z, hp_up.at[s - 1])
            h_state["down"] = cp.start(hp.at[zof(-s), c], hp_dn.at[s - 1], down_z, hp_dn.at[s - 1])

    b_in, o_in = [], []

    def lo_second(k):
        dz, dc = order[k]
        zs, cs = zof(dz), (c + dc) % 2
        a_in[k][0].wait_recv()
        add_into(lo.at[zs, cs, yof(1), 0:half], lo_half_up.at[k])
        first = cp.start(lo.at[zs, cs, yof(1)], lo_up.at[k], up_y, lo_up.at[k])
        a_in[k][1].wait_recv()
        add_into(lo.at[zs, cs, yof(-1), half:TOK], lo_half_dn.at[k])
        b_in.append((first, cp.start(lo.at[zs, cs, yof(-1)], lo_dn.at[k], down_y, lo_dn.at[k])))

    def lo_third(k):
        dz, dc = order[k]
        zs, cs = zof(dz), (c + dc) % 2
        for copy in b_in[k]:
            copy.wait_recv()
        add_into(lo.at[zs, cs, y], lo_up.at[k], lo_dn.at[k])
        mine = out.at[:, quarter(z * 2 + c)]
        if (dz, dc) == (0, 0):
            o_in.append(cp.local(lo.at[zs, cs, y], mine))
        else:
            o_in.append(cp.start(lo.at[zs, cs, y], mine, device(x, y, zs, cs), out.at[:, quarter(zof(-dz) * 2 + cs)]))

    d_state = {}

    def d_step(s):
        if s == 0:
            d_in[0].wait_recv()
            add_into(dw.at[xof(1), 0 : EXPERTS // 2], dw_half_up)
            d_state["up"] = cp.start(dw.at[xof(1)], dw_up, up_x, dw_up)
            d_in[1].wait_recv()
            add_into(dw.at[xof(-1), EXPERTS // 2 : EXPERTS], dw_half_dn)
            d_state["down"] = cp.start(dw.at[xof(-1)], dw_dn, down_x, dw_dn)
            return
        d_state["up"].wait_recv()
        d_state["down"].wait_recv()
        span = ROWS * 4

        def turn(e, carry):
            value = dw[x, e].astype(jnp.float32) + dw_up[e].astype(jnp.float32) + dw_dn[e].astype(jnp.float32)
            for j in range(COLS // 128):
                wide[j, pl.ds(e, span, stride=EXPERTS), :] = value[:, j * 128 : (j + 1) * 128]
            return carry

        lax.fori_loop(0, EXPERTS, turn, 0)

        def narrow(i, carry):
            rows = pl.ds(pl.multiple_of(i * EXPERTS, EXPERTS), EXPERTS)
            for j in range(COLS // 128):
                turned[i // ROWS, i % ROWS, :, j * 128 : (j + 1) * 128] = wide[j, rows, :].astype(jnp.bfloat16)
            return carry

        lax.fori_loop(0, span, narrow, 0)
        for dl, dc in ((1, 0), (1, 1), (0, 1)):
            ol, oc = (zl + dl) % 2, (c + dc) % 2
            there = ol * 2 + oc
            o_in.append(cp.start(turned.at[there], wout.at[:, :, quarter(here)], device(x, y, (z // 2) * 2 + ol, oc), wout.at[:, :, quarter(there)]))
        o_in.append(cp.local(turned.at[here], wout.at[:, :, quarter(here)]))

    h_step(4)
    steps = len(order)
    for k in range(steps):
        lo_second(k)
        if k >= 2:
            lo_third(k - 2)
        if k in (3, 6, 9, 12):
            h_step(4 - k // 3)
        if k == 4:
            d_step(0)
        if k == 10:
            d_step(1)
    for dy in (1, 3, 2):
        oy = yof(dy)
        o_in.append(cp.start(hp.at[z, c, oy], hout.at[y], device(x, oy, z, c), hout.at[yof(-dy)]))
    o_in.append(cp.local(hp.at[z, c, y], hout.at[y]))
    lo_third(steps - 2)
    lo_third(steps - 1)
    for copy in o_in:
        if copy.is_remote:
            copy.wait_recv()
        else:
            copy.wait()
    cp.drain()


def body(hidden_rows, out_grad, expert_weights, need_lists, block_pick, owner_slot):
    bf16 = jnp.bfloat16
    shape = jax.ShapeDtypeStruct
    anywhere = pl.BlockSpec(memory_space=pl.ANY)
    vmem = pl.BlockSpec(memory_space=pltpu.VMEM)
    x = lax.axis_index("dev") // 16

    span = ROWS * 4
    ht = hidden_rows.reshape(TOK, NX, 2, NY, NC, ROWS).transpose(3, 1, 2, 4, 5, 0).reshape(NY, GROUP, TOK)
    wt = expert_weights.transpose(1, 0, 2)
    pick = jnp.broadcast_to(jnp.pad(block_pick, (0, 126))[None, :], (8, 128))

    wg, hg, gg, picks = pl.pallas_call(
        gather_kernel,
        out_shape=(
            shape((NX, EXPERTS, span, COLS), bf16),
            shape((NZ, NC, NY, GROUP, TOK), bf16),
            shape((NZ, NC, NY, TOK, COLS), bf16),
            shape((NZ, NC, NY, 8, 128), jnp.int32),
        ),
        in_specs=[anywhere] * 4,
        out_specs=(anywhere,) * 4,
        scratch_shapes=[
            pltpu.VMEM((4, ROWS, EXPERTS, COLS), bf16),
            pltpu.VMEM((COLS // 128, span * EXPERTS, 128), jnp.float32),
            pltpu.VMEM((EXPERTS, span, COLS), bf16),
            pltpu.SemaphoreType.DMA((160,)),
            pltpu.SemaphoreType.DMA((160,)),
        ],
        compiler_params=pltpu.CompilerParams(collective_id=0, has_side_effects=True, vmem_limit_bytes=VMEM_LIMIT),
        name="gather",
    )(wt, ht, out_grad, pick)

    needs = need_lists.reshape(4, NX, 2, NY, NC, 2)
    needs = lax.dynamic_index_in_dim(needs, x, 1, keepdims=False).transpose(0, 1, 3, 2, 4).reshape(-1, 2)
    ids = jnp.arange(EXPERTS, dtype=jnp.int32)
    known = jnp.sum(jnp.where(needs[:, :, None] == ids, owner_slot[None, None, :], 0), axis=2)
    chosen = picks.reshape(-1, 8, 128)[:, 0, 0:2]
    slots = jnp.where(chosen == 0, known[:, 0:1], known[:, 1:2]).reshape(-1)

    sources = NZ * NC * NY
    each = 1
    one = lambda rows: pl.BlockSpec((each, rows, 256), lambda i, s: (i, 0, 0))
    whole = lambda: pl.BlockSpec((NX, EXPERTS, span, COLS), lambda i, s: (0, 0, 0, 0), pipeline_mode=pl.Buffered(1))
    lo, hp, dw = pl.pallas_call(
        compute_kernel,
        grid_spec=pltpu.PrefetchScalarGridSpec(
            num_scalar_prefetch=1,
            grid=(sources // each,),
            in_specs=[whole(), one(GROUP), one(TOK)],
            out_specs=(one(TOK), one(GROUP), whole()),
            scratch_shapes=[pltpu.VMEM((NX, EXPERTS, span, COLS), jnp.float32)],
        ),
        out_shape=(
            shape((sources, TOK, COLS), bf16),
            shape((sources, GROUP, TOK), bf16),
            shape((NX, EXPERTS, span, COLS), bf16),
        ),
        compiler_params=pltpu.CompilerParams(vmem_limit_bytes=VMEM_LIMIT),
        name="compute",
    )(slots, wg, hg.reshape(sources, GROUP, TOK), gg.reshape(sources, TOK, COLS))

    half = TOK // 2
    pieces = len(OFFSETS)
    layer_out, hidden, weight_grad = pl.pallas_call(
        scatter_kernel,
        out_shape=(
            shape((TOK, 4096), bf16),
            shape((NY, GROUP, TOK), bf16),
            shape((ROWS, EXPERTS, 1024), bf16),
        ),
        in_specs=[vmem] * 3,
        out_specs=(anywhere,) * 3,
        scratch_shapes=[
            pltpu.VMEM((pieces, half, COLS), bf16),
            pltpu.VMEM((pieces, half, COLS), bf16),
            pltpu.VMEM((pieces, TOK, COLS), bf16),
            pltpu.VMEM((pieces, TOK, COLS), bf16),
            pltpu.VMEM((NZ, NY, GROUP, TOK), bf16),
            pltpu.VMEM((4, NY, GROUP, TOK), bf16),
            pltpu.VMEM((4, NY, GROUP, TOK), bf16),
            pltpu.VMEM((EXPERTS // 2, span, COLS), bf16),
            pltpu.VMEM((EXPERTS // 2, span, COLS), bf16),
            pltpu.VMEM((EXPERTS, span, COLS), bf16),
            pltpu.VMEM((EXPERTS, span, COLS), bf16),
            pltpu.VMEM((COLS // 128, span * EXPERTS, 128), jnp.float32),
            pltpu.VMEM((4, ROWS, EXPERTS, COLS), bf16),
            pltpu.SemaphoreType.DMA((128,)),
            pltpu.SemaphoreType.DMA((128,)),
        ],
        compiler_params=pltpu.CompilerParams(collective_id=1, has_side_effects=True, vmem_limit_bytes=VMEM_LIMIT),
        name="scatter",
    )(
        lo.reshape(NZ, NC, NY, TOK, COLS),
        hp.reshape(NZ, NC, NY, GROUP, TOK),
        dw,
    )
    hidden_grad = hidden.reshape(NY, NX, 2, NC, ROWS, TOK).transpose(5, 1, 2, 0, 3, 4).reshape(TOK, -1)
    return layer_out, hidden_grad, weight_grad.transpose(1, 0, 2)


def solution(mesh):
    return jax.shard_map(
        body,
        mesh=mesh,
        in_specs=(
            P(("outer", "dev"), None),
            P(("outer", "dev"), None),
            P(None, "dev", "outer"),
            P(),
            P(("outer", "dev")),
            P(),
        ),
        out_specs=(P(("outer", "dev"), None), P(("outer", "dev"), None), P(None, "dev", "outer")),
        check_vma=False,
    )
```

```python
import functools

import jax
import jax.numpy as jnp
from jax import lax
from jax.experimental import pallas as pl
from jax.experimental.pallas import tpu as pltpu
from jax.sharding import PartitionSpec as P

MESH = pl.DeviceIdType.MESH
BLOCK = 128
NX, NY, NZ, NC = 4, 4, 8, 2
ROWS = 12
SPAN = 4 * ROWS
GROUP = 192
COLS = 256
TOK = 256
EXPERTS = 64
VMEM_LIMIT = 60 * 2**20
OFFSETS = [(dz, dc) for dz in (0, 1, -1, 2, -2, 3, -3, 4) for dc in (0, 1)]


WINDOW = 6
HSTEPS = (6, 9, 12, 15)
H_BACK = (2, 6, 10, 13)


def coords():
    o, d = lax.axis_index("outer"), lax.axis_index("dev")
    return d // 16, (d // 2) % 4, o * 2 + (d // 8) % 2, d % 2


def device(x, y, z, c):
    return (z // 2, x * 16 + (z % 2) * 8 + y * 2 + c)


class Copies:
    def __init__(self, send, recv):
        self.send, self.recv, self.used, self.pending = send, recv, 0, []

    def start(self, src, dst, target, land):
        n = self.used
        self.used += 1
        copy = pltpu.make_async_remote_copy(src, dst, self.send.at[n], self.recv.at[n], device_id=target, device_id_type=MESH)
        copy.start()
        self.pending.append(copy)
        back = pltpu.make_async_remote_copy(land, land, self.send.at[n], self.recv.at[n], device_id=target, device_id_type=MESH)
        return back

    def local(self, src, dst):
        n = self.used
        self.used += 1
        copy = pltpu.make_async_copy(src, dst, self.recv.at[n])
        copy.start()
        return copy

    def drain(self):
        for copy in self.pending:
            copy.wait_send()


def greet(x, y, z, c):
    barrier = pltpu.get_barrier_semaphore()
    others = [(x, y, (z + dz + NZ) % NZ, (c + dc) % 2) for dz, dc in OFFSETS[1:]]
    others += [(x, (y + dy) % NY, z, c) for dy in (1, 2, 3)]
    others += [((x + dx) % NX, y, z, c) for dx in (1, 3)]
    for other in others:
        pl.semaphore_signal(barrier, inc=1, device_id=device(*other), device_id_type=MESH)
    pl.semaphore_wait(barrier, len(others))


def quarter(q):
    return pl.ds(pl.multiple_of(q * COLS, COLS), COLS)


def gather_kernel(w, h, g, pick, wg, hg, gg, picks, landed, wide, turned, send, recv):
    x, y, z, c = coords()
    greet(x, y, z, c)
    cp = Copies(send, recv)
    zof = lambda d: (z + d + NZ) % NZ
    yof = lambda d: (y + d + NY) % NY
    xof = lambda d: (x + d + NX) % NX
    zl = z % 2
    here = zl * 2 + c

    h1 = []
    for dy in (1, 3, 2):
        oy = yof(dy)
        h1.append(cp.start(h.at[oy], hg.at[z, c, y], device(x, oy, z, c), hg.at[z, c, yof(-dy)]))
        h1.append(cp.start(pick, picks.at[z, c, y], device(x, oy, z, c), picks.at[z, c, yof(-dy)]))
    h1.append(cp.local(h.at[y], hg.at[z, c, y]))
    h1.append(cp.local(pick, picks.at[z, c, y]))
    w1 = []
    for dl, dc in ((1, 0), (1, 1), (0, 1)):
        ol, oc = (zl + dl) % 2, (c + dc) % 2
        there = ol * 2 + oc
        w1.append(cp.start(w.at[:, :, quarter(there)], landed.at[here], device(x, y, (z // 2) * 2 + ol, oc), landed.at[there]))
    w1.append(cp.local(w.at[:, :, quarter(here)], landed.at[here]))

    g1 = []

    def g_start(k):
        dz, dc = OFFSETS[k]
        if (dz, dc) == (0, 0):
            g1.append(cp.local(g.at[:, quarter(z * 2 + c)], gg.at[z, c, y]))
            return
        oz, oc = zof(dz), (c + dc) % 2
        g1.append(cp.start(g.at[:, quarter(oz * 2 + oc)], gg.at[z, c, y], device(x, y, oz, oc), gg.at[zof(-dz), oc, y]))

    def wait(copy):
        if copy.is_remote:
            copy.wait_recv()
        else:
            copy.wait()

    up_z, down_z = device(x, y, zof(1), c), device(x, y, zof(-1), c)
    up_y, down_y = device(x, yof(1), z, c), device(x, yof(-1), z, c)
    up_x, down_x = device(xof(1), y, z, c), device(xof(-1), y, z, c)
    sibling = device(x, y, z, (c + 1) % 2)

    h_state = []
    h_sib = []

    def h_send(pairs, target, back):
        for ref, at, land in pairs:
            back.append(cp.start(ref.at[at], ref.at[at], target, ref.at[land]))

    def h_step(s):
        for copy in h1 if s == 0 else list(h_state):
            wait(copy)
        h_state.clear()
        behind, ahead = zof(-s), zof(s)
        if s < 3:
            h_send([(hg, (behind, c), (zof(-s - 1), c)), (picks, (behind, c), (zof(-s - 1), c))], up_z, h_state)
            h_send([(hg, (ahead, c), (zof(s + 1), c)), (picks, (ahead, c), (zof(s + 1), c))], down_z, h_state)
        elif s == 3:
            low, high = slice(0, 2), slice(2, 4)
            h_send([(hg, (behind, c, low), (zof(-4), c, low)), (picks, (behind, c, low), (zof(-4), c, low))], up_z, h_state)
            h_send([(hg, (ahead, c, high), (zof(4), c, high)), (picks, (ahead, c, high), (zof(4), c, high))], down_z, h_state)
        for zz in [behind] if s in (0, 4) else [behind, ahead]:
            h_send([(r, (zz, c), (zz, (c + 1) % 2)) for r in (hg, picks)], sibling, h_sib)

    w_state = {}
    bf16 = jnp.bfloat16
    span = SPAN

    def w_step(s):
        if s == 0:
            for copy in w1:
                wait(copy)

            def widen(i, carry):
                q, r = i // ROWS, i % ROWS
                rows = pl.ds(pl.multiple_of(i * EXPERTS, EXPERTS), EXPERTS)
                for j in range(COLS // 128):
                    wide[j, rows, :] = landed[q, r, :, j * 128 : (j + 1) * 128].astype(jnp.float32)
                return carry

            lax.fori_loop(0, span, widen, 0)

            def turn(e, carry):
                for j in range(COLS // 128):
                    turned[e, :, j * 128 : (j + 1) * 128] = wide[j, pl.ds(e, span, stride=EXPERTS), :].astype(bf16)
                return carry

            lax.fori_loop(0, EXPERTS, turn, 0)
            w_state["up"] = cp.start(turned, wg.at[x], up_x, wg.at[xof(-1)])
            w_state["down"] = cp.start(turned, wg.at[x], down_x, wg.at[xof(1)])
            w_state["own"] = cp.local(turned, wg.at[x])
        else:
            wait(w_state["up"])
            wait(w_state["down"])
            if s == 1:
                low, high = slice(0, EXPERTS // 2), slice(EXPERTS // 2, EXPERTS)
                w_state["up"] = cp.start(wg.at[xof(-1), low], wg.at[xof(-1), low], up_x, wg.at[xof(-2), low])
                w_state["down"] = cp.start(wg.at[xof(1), high], wg.at[xof(1), high], down_x, wg.at[xof(2), high])
            else:
                wait(w_state["own"])

    g2, g3 = [], []
    half = TOK // 2

    def g_first(k):
        wait(g1[k])
        dz, dc = OFFSETS[k]
        zs, cs = zof(-dz), (c + dc) % 2
        mine = gg.at[zs, cs, y]
        g2.append((cp.start(mine, mine, up_y, gg.at[zs, cs, yof(-1)]), cp.start(mine, mine, down_y, gg.at[zs, cs, yof(1)])))

    def g_second(k):
        dz, dc = OFFSETS[k]
        zs, cs = zof(-dz), (c + dc) % 2
        for copy in g2[k]:
            wait(copy)
        below = gg.at[zs, cs, yof(-1), 0:half]
        above = gg.at[zs, cs, yof(1), half:TOK]
        g3.append(cp.start(below, below, up_y, gg.at[zs, cs, yof(-2), 0:half]))
        g3.append(cp.start(above, above, down_y, gg.at[zs, cs, yof(2), half:TOK]))

    steps = len(OFFSETS)
    for k in range(WINDOW):
        g_start(k)
    h_step(0)
    g_first(0)
    g_first(1)
    for k in range(2, steps):
        if k - 2 + WINDOW < steps:
            g_start(k - 2 + WINDOW)
        g_first(k)
        if k == 3:
            w_step(0)
        g_second(k - 2)
        if k in HSTEPS:
            h_step(HSTEPS.index(k) + 1)
        if k == 12:
            w_step(1)
    g_second(steps - 2)
    g_second(steps - 1)
    w_step(2)
    for copy in g3 + h_sib:
        wait(copy)
    cp.drain()


def compute_kernel(slots, h, g, dw, acc):
    step = pl.program_id(0)

    @pl.when(step == 0)
    def _():
        def clear(e, carry):
            for j in range(NX):
                acc[j, e] = jnp.zeros((SPAN, COLS), jnp.float32)
            return carry

        lax.fori_loop(0, EXPERTS, clear, 0)

    for n in range(h.shape[0]):
        for b in range(TOK // BLOCK):
            slot = slots[(step * h.shape[0] + n) * (TOK // BLOCK) + b]
            tokens = slice(b * BLOCK, (b + 1) * BLOCK)
            outer = jnp.dot(h[n, :, tokens], g[n, tokens, :], preferred_element_type=jnp.float32)
            for j in range(NX):
                acc[j, slot] += outer[j * SPAN : (j + 1) * SPAN]

    @pl.when(step == pl.num_programs(0) - 1)
    def _():
        def empty(e, carry):
            for j in range(NX):
                dw[j, e] = acc[j, e].astype(jnp.bfloat16)
            return carry

        lax.fori_loop(0, EXPERTS, empty, 0)


def add_into(dst, *others):
    lead = dst.shape[:-2]
    rows = dst.shape[-2]
    cut = min(rows, 64)
    per = rows // cut
    total = per
    for n in lead:
        total *= n

    def one(i, carry):
        where, rest = [], i // per
        for n in reversed(lead):
            where.insert(0, rest % n)
            rest = rest // n
        at = tuple(where) + (pl.ds(pl.multiple_of((i % per) * cut, cut), cut), slice(None))
        value = dst[at].astype(jnp.float32)
        for other in others:
            value += other[at].astype(jnp.float32)
        dst[at] = value.astype(jnp.bfloat16)
        return carry

    lax.fori_loop(0, total, one, 0)


def scatter_kernel(slots, w, h, g, dw, out, hout, wout, hv, gv, lo_half_up, lo_half_dn, lo_up, lo_dn, sib, hp_up, hp_dn, dw_half_up, dw_half_dn, dw_up, dw_dn, wide, turned, send, recv):
    x, y, z, c = coords()
    cp = Copies(send, recv)
    zof = lambda d: (z + d + NZ) % NZ
    yof = lambda d: (y + d + NY) % NY
    xof = lambda d: (x + d + NX) % NX
    zl = z % 2
    here = zl * 2 + c
    up_z, down_z = device(x, y, zof(1), c), device(x, y, zof(-1), c)
    up_y, down_y = device(x, yof(1), z, c), device(x, yof(-1), z, c)
    up_x, down_x = device(xof(1), y, z, c), device(xof(-1), y, z, c)
    sibling = device(x, y, z, (c + 1) % 2)
    half = TOK // 2
    low, high = slice(0, EXPERTS // 2), slice(EXPERTS // 2, EXPERTS)
    order = list(reversed(OFFSETS))
    places = [(zof(dz), (c + dc) % 2) for dz, dc in order]

    loads = [(cp.local(h.at[zs, cs], hv.at[zs, cs]), cp.local(g.at[zs, cs], gv.at[zs, cs])) for zs, cs in places]
    greet(x, y, z, c)
    d_in = (
        cp.start(dw.at[xof(2), low], dw_half_up, up_x, dw_half_up),
        cp.start(dw.at[xof(2), high], dw_half_dn, down_x, dw_half_dn),
    )

    def products(k):
        zs, cs = places[k]
        for copy in loads[k]:
            copy.wait()

        def one(i, carry):
            results = []
            for b in range(TOK // BLOCK):
                slot = slots[((zs * NC + cs) * NY + i) * (TOK // BLOCK) + b]
                weight = jnp.concatenate([w[j, slot] for j in range(NX)], axis=0)
                tokens = slice(b * BLOCK, (b + 1) * BLOCK)
                hid = hv[zs, cs, i, :, tokens]
                cot = gv[zs, cs, i, tokens, :]
                lo = lax.dot_general(hid, weight, (((0,), (0,)), ((), ())), preferred_element_type=jnp.float32)
                hg = lax.dot_general(weight, cot, (((1,), (1,)), ((), ())), preferred_element_type=jnp.float32)
                results.append((tokens, lo, hg))
            for tokens, lo, hg in results:
                gv[zs, cs, i, tokens, :] = lo.astype(jnp.bfloat16)
                hv[zs, cs, i, :, tokens] = hg.astype(jnp.bfloat16)
            return carry

        lax.fori_loop(0, NY, one, 0)

    sib_in, a_in, b_in, o_in = {}, [], [], []

    def lo_first(k):
        zs, cs = places[k]
        a_in.append((
            cp.start(gv.at[zs, cs, yof(2), 0:half], lo_half_up.at[k], up_y, lo_half_up.at[k]),
            cp.start(gv.at[zs, cs, yof(2), half:TOK], lo_half_dn.at[k], down_y, lo_half_dn.at[k]),
        ))
        dz, dc = order[k]
        if dc:
            sib_in[dz] = cp.start(hv.at[zs, cs], sib.at[zs], sibling, sib.at[zs])

    def lo_second(k):
        zs, cs = places[k]
        a_in[k][0].wait_recv()
        add_into(gv.at[zs, cs, yof(1), 0:half], lo_half_up.at[k])
        first = cp.start(gv.at[zs, cs, yof(1)], lo_up.at[k], up_y, lo_up.at[k])
        a_in[k][1].wait_recv()
        add_into(gv.at[zs, cs, yof(-1), half:TOK], lo_half_dn.at[k])
        b_in.append((first, cp.start(gv.at[zs, cs, yof(-1)], lo_dn.at[k], down_y, lo_dn.at[k])))

    def lo_third(k):
        dz, dc = order[k]
        zs, cs = places[k]
        for copy in b_in[k]:
            copy.wait_recv()
        add_into(gv.at[zs, cs, y], lo_up.at[k], lo_dn.at[k])
        mine = out.at[:, quarter(z * 2 + c)]
        if (dz, dc) == (0, 0):
            o_in.append(cp.local(gv.at[zs, cs, y], mine))
        else:
            o_in.append(cp.start(gv.at[zs, cs, y], mine, device(x, y, zs, cs), out.at[:, quarter(zof(-dz) * 2 + cs)]))

    h_state = {}

    def h_step(s):
        for d in (4,) if s == 4 else (s, -s) if s else (0,):
            sib_in[d].wait_recv()
        if s < 4:
            h_state["up"].wait_recv()
            h_state["down"].wait_recv()
        first, last = slice(0, 2), slice(2, 4)
        if s == 4:
            add_into(hv.at[zof(4), c], sib.at[zof(4)])
            h_state["up"] = cp.start(hv.at[zof(4), c, first], hp_up.at[3, first], up_z, hp_up.at[3, first])
            h_state["down"] = cp.start(hv.at[zof(4), c, last], hp_dn.at[3, last], down_z, hp_dn.at[3, last])
            return
        if s == 3:
            add_into(hv.at[zof(3), c, first], sib.at[zof(3), first], hp_up.at[3, first])
            add_into(hv.at[zof(3), c, last], sib.at[zof(3), last])
            add_into(hv.at[zof(-3), c, first], sib.at[zof(-3), first])
            add_into(hv.at[zof(-3), c, last], sib.at[zof(-3), last], hp_dn.at[3, last])
        elif s > 0:
            add_into(hv.at[zof(s), c], sib.at[zof(s)], hp_up.at[s])
            add_into(hv.at[zof(-s), c], sib.at[zof(-s)], hp_dn.at[s])
        else:
            add_into(hv.at[z, c], sib.at[z], hp_up.at[0], hp_dn.at[0])
        if s > 0:
            h_state["up"] = cp.start(hv.at[zof(s), c], hp_up.at[s - 1], up_z, hp_up.at[s - 1])
            h_state["down"] = cp.start(hv.at[zof(-s), c], hp_dn.at[s - 1], down_z, hp_dn.at[s - 1])

    d_state = {}

    def d_step(s):
        if s == 0:
            d_in[0].wait_recv()
            add_into(dw.at[xof(1), low], dw_half_up)
            d_state["up"] = cp.start(dw.at[xof(1)], dw_up, up_x, dw_up)
            d_in[1].wait_recv()
            add_into(dw.at[xof(-1), high], dw_half_dn)
            d_state["down"] = cp.start(dw.at[xof(-1)], dw_dn, down_x, dw_dn)
            return
        d_state["up"].wait_recv()
        d_state["down"].wait_recv()

        def turn(e, carry):
            value = dw[x, e].astype(jnp.float32) + dw_up[e].astype(jnp.float32) + dw_dn[e].astype(jnp.float32)
            for j in range(COLS // 128):
                wide[j, pl.ds(e, SPAN, stride=EXPERTS), :] = value[:, j * 128 : (j + 1) * 128]
            return carry

        lax.fori_loop(0, EXPERTS, turn, 0)

        def narrow(i, carry):
            rows = pl.ds(pl.multiple_of(i * EXPERTS, EXPERTS), EXPERTS)
            for j in range(COLS // 128):
                turned[i // ROWS, i % ROWS, :, j * 128 : (j + 1) * 128] = wide[j, rows, :].astype(jnp.bfloat16)
            return carry

        lax.fori_loop(0, SPAN, narrow, 0)
        for dl, dc in ((1, 0), (1, 1), (0, 1)):
            ol, oc = (zl + dl) % 2, (c + dc) % 2
            there = ol * 2 + oc
            o_in.append(cp.start(turned.at[there], wout.at[:, :, quarter(here)], device(x, y, (z // 2) * 2 + ol, oc), wout.at[:, :, quarter(there)]))
        o_in.append(cp.local(turned.at[here], wout.at[:, :, quarter(here)]))

    steps = len(order)
    for k in range(steps):
        products(k)
        lo_first(k)
        if k >= 1:
            lo_second(k - 1)
        if k >= 3:
            lo_third(k - 3)
        if k in H_BACK:
            h_step(4 - H_BACK.index(k))
        if k == 7:
            d_step(0)
    lo_second(steps - 1)
    lo_third(steps - 3)
    d_step(1)
    lo_third(steps - 2)
    h_step(0)
    for dy in (1, 3, 2):
        oy = yof(dy)
        o_in.append(cp.start(hv.at[z, c, oy], hout.at[y], device(x, oy, z, c), hout.at[yof(-dy)]))
    o_in.append(cp.local(hv.at[z, c, y], hout.at[y]))
    lo_third(steps - 1)
    for copy in o_in:
        if copy.is_remote:
            copy.wait_recv()
        else:
            copy.wait()
    cp.drain()


def body(hidden_rows, out_grad, expert_weights, need_lists, block_pick, owner_slot):
    bf16 = jnp.bfloat16
    shape = jax.ShapeDtypeStruct
    anywhere = pl.BlockSpec(memory_space=pl.ANY)
    vmem = pl.BlockSpec(memory_space=pltpu.VMEM)
    x = lax.axis_index("dev") // 16

    ht = hidden_rows.reshape(TOK, NX, 2, NY, NC, ROWS).transpose(3, 1, 2, 4, 5, 0).reshape(NY, GROUP, TOK)
    wt = expert_weights.transpose(1, 0, 2)
    pick = jnp.broadcast_to(jnp.pad(block_pick, (0, 126))[None, :], (8, 128))

    wg, hg, gg, picks = pl.pallas_call(
        gather_kernel,
        out_shape=(
            shape((NX, EXPERTS, SPAN, COLS), bf16),
            shape((NZ, NC, NY, GROUP, TOK), bf16),
            shape((NZ, NC, NY, TOK, COLS), bf16),
            shape((NZ, NC, NY, 8, 128), jnp.int32),
        ),
        in_specs=[anywhere] * 4,
        out_specs=(anywhere,) * 4,
        scratch_shapes=[
            pltpu.VMEM((4, ROWS, EXPERTS, COLS), bf16),
            pltpu.VMEM((COLS // 128, SPAN * EXPERTS, 128), jnp.float32),
            pltpu.VMEM((EXPERTS, SPAN, COLS), bf16),
            pltpu.SemaphoreType.DMA((160,)),
            pltpu.SemaphoreType.DMA((160,)),
        ],
        compiler_params=pltpu.CompilerParams(collective_id=0, has_side_effects=True, vmem_limit_bytes=VMEM_LIMIT),
        name="gather",
    )(wt, ht, out_grad, pick)

    needs = need_lists.reshape(4, NX, 2, NY, NC, 2)
    needs = lax.dynamic_index_in_dim(needs, x, 1, keepdims=False).transpose(0, 1, 3, 2, 4).reshape(-1, 2)
    ids = jnp.arange(EXPERTS, dtype=jnp.int32)
    known = jnp.sum(jnp.where(needs[:, :, None] == ids, owner_slot[None, None, :], 0), axis=2)
    chosen = picks.reshape(-1, 8, 128)[:, 0, 0:2]
    slots = jnp.where(chosen == 0, known[:, 0:1], known[:, 1:2]).reshape(-1)

    sources = NZ * NC * NY
    each = 2
    one = lambda rows: pl.BlockSpec((each, rows, 256), lambda i, s: (i, 0, 0))
    dw = pl.pallas_call(
        compute_kernel,
        grid_spec=pltpu.PrefetchScalarGridSpec(
            num_scalar_prefetch=1,
            grid=(sources // each,),
            in_specs=[one(GROUP), one(TOK)],
            out_specs=pl.BlockSpec((NX, EXPERTS, SPAN, COLS), lambda i, s: (0, 0, 0, 0), pipeline_mode=pl.Buffered(1)),
            scratch_shapes=[pltpu.VMEM((NX, EXPERTS, SPAN, COLS), jnp.float32)],
        ),
        out_shape=shape((NX, EXPERTS, SPAN, COLS), bf16),
        compiler_params=pltpu.CompilerParams(vmem_limit_bytes=VMEM_LIMIT),
        name="weight_gradient",
    )(slots, hg.reshape(sources, GROUP, TOK), gg.reshape(sources, TOK, COLS))

    half = TOK // 2
    pieces = len(OFFSETS)
    layer_out, hidden, weight_grad = pl.pallas_call(
        scatter_kernel,
        out_shape=(
            shape((TOK, 4096), bf16),
            shape((NY, GROUP, TOK), bf16),
            shape((ROWS, EXPERTS, 1024), bf16),
        ),
        in_specs=[pl.BlockSpec(memory_space=pltpu.SMEM), vmem, anywhere, anywhere, vmem],
        out_specs=(anywhere,) * 3,
        scratch_shapes=[
            pltpu.VMEM((NZ, NC, NY, GROUP, TOK), bf16),
            pltpu.VMEM((NZ, NC, NY, TOK, COLS), bf16),
            pltpu.VMEM((pieces, half, COLS), bf16),
            pltpu.VMEM((pieces, half, COLS), bf16),
            pltpu.VMEM((pieces, TOK, COLS), bf16),
            pltpu.VMEM((pieces, TOK, COLS), bf16),
            pltpu.VMEM((NZ, NY, GROUP, TOK), bf16),
            pltpu.VMEM((4, NY, GROUP, TOK), bf16),
            pltpu.VMEM((4, NY, GROUP, TOK), bf16),
            pltpu.VMEM((EXPERTS // 2, SPAN, COLS), bf16),
            pltpu.VMEM((EXPERTS // 2, SPAN, COLS), bf16),
            pltpu.VMEM((EXPERTS, SPAN, COLS), bf16),
            pltpu.VMEM((EXPERTS, SPAN, COLS), bf16),
            pltpu.VMEM((COLS // 128, SPAN * EXPERTS, 128), jnp.float32),
            pltpu.VMEM((4, ROWS, EXPERTS, COLS), bf16),
            pltpu.SemaphoreType.DMA((160,)),
            pltpu.SemaphoreType.DMA((160,)),
        ],
        compiler_params=pltpu.CompilerParams(collective_id=1, has_side_effects=True, vmem_limit_bytes=VMEM_LIMIT),
        name="scatter",
    )(slots, wg, hg, gg, dw)
    hidden_grad = hidden.reshape(NY, NX, 2, NC, ROWS, TOK).transpose(5, 1, 2, 0, 3, 4).reshape(TOK, -1)
    return layer_out, hidden_grad, weight_grad.transpose(1, 0, 2)


def solution(mesh):
    return jax.shard_map(
        body,
        mesh=mesh,
        in_specs=(
            P(("outer", "dev"), None),
            P(("outer", "dev"), None),
            P(None, "dev", "outer"),
            P(),
            P(("outer", "dev")),
            P(),
        ),
        out_specs=(P(("outer", "dev"), None), P(("outer", "dev"), None), P(None, "dev", "outer")),
        check_vma=False,
    )
```

```python
import functools

import jax
import jax.numpy as jnp
from jax import lax
from jax.experimental import pallas as pl
from jax.experimental.pallas import tpu as pltpu
from jax.sharding import PartitionSpec as P

MESH = pl.DeviceIdType.MESH
BLOCK = 128
NX, NY, NZ, NC = 4, 4, 8, 2
ROWS = 12
SPAN = 4 * ROWS
GROUP = 192
COLS = 256
TOK = 256
EXPERTS = 64
VMEM_LIMIT = 60 * 2**20
OFFSETS = [(dz, dc) for dz in (0, 1, -1, 2, -2, 3, -3, 4) for dc in (0, 1)]


WINDOW = 6
HSTEPS = (5, 8, 11)
WEIGH = (0, 0, 0, 0, 1, 2, 3, 4, 5, 6, 7, 8, 9, 10, 11, 12)
H_BACK = (2, 6, 10, 13)


def coords():
    o, d = lax.axis_index("outer"), lax.axis_index("dev")
    return d // 16, (d // 2) % 4, o * 2 + (d // 8) % 2, d % 2


def device(x, y, z, c):
    return (z // 2, x * 16 + (z % 2) * 8 + y * 2 + c)


class Copies:
    def __init__(self, send, recv):
        self.send, self.recv, self.used, self.pending = send, recv, 0, []

    def start(self, src, dst, target, land):
        n = self.used
        self.used += 1
        copy = pltpu.make_async_remote_copy(src, dst, self.send.at[n], self.recv.at[n], device_id=target, device_id_type=MESH)
        copy.start()
        self.pending.append(copy)
        back = pltpu.make_async_remote_copy(land, land, self.send.at[n], self.recv.at[n], device_id=target, device_id_type=MESH)
        return back

    def local(self, src, dst):
        n = self.used
        self.used += 1
        copy = pltpu.make_async_copy(src, dst, self.recv.at[n])
        copy.start()
        return copy

    def drain(self):
        for copy in self.pending:
            copy.wait_send()


def greet(x, y, z, c):
    barrier = pltpu.get_barrier_semaphore()
    others = [(x, y, (z + dz + NZ) % NZ, (c + dc) % 2) for dz, dc in OFFSETS[1:]]
    others += [(x, (y + dy) % NY, z, c) for dy in (1, 2, 3)]
    others += [((x + dx) % NX, y, z, c) for dx in (1, 3)]
    for other in others:
        pl.semaphore_signal(barrier, inc=1, device_id=device(*other), device_id_type=MESH)
    pl.semaphore_wait(barrier, len(others))


def quarter(q):
    return pl.ds(pl.multiple_of(q * COLS, COLS), COLS)


def gather_kernel(chain, w, h, g, pick, wg, hg_out, gg_out, picks_out, dw_out, hg, gg, picks, sums, dw, landed, wide, turned, send, recv):
    x, y, z, c = coords()
    greet(x, y, z, c)
    cp = Copies(send, recv)
    zof = lambda d: (z + d + NZ) % NZ
    yof = lambda d: (y + d + NY) % NY
    xof = lambda d: (x + d + NX) % NX
    zl = z % 2
    here = zl * 2 + c

    h1 = []
    for dy in (1, 3, 2):
        oy = yof(dy)
        h1.append(cp.start(h.at[oy], hg.at[z, c, y], device(x, oy, z, c), hg.at[z, c, yof(-dy)]))
        h1.append(cp.start(pick, picks.at[z, c, y], device(x, oy, z, c), picks.at[z, c, yof(-dy)]))
    h1.append(cp.local(h.at[y], hg.at[z, c, y]))
    h1.append(cp.local(pick, picks.at[z, c, y]))
    w1 = []
    for dl, dc in ((1, 0), (1, 1), (0, 1)):
        ol, oc = (zl + dl) % 2, (c + dc) % 2
        there = ol * 2 + oc
        w1.append(cp.start(w.at[:, :, quarter(there)], landed.at[here], device(x, y, (z // 2) * 2 + ol, oc), landed.at[there]))
    w1.append(cp.local(w.at[:, :, quarter(here)], landed.at[here]))

    g1 = []

    def g_start(k):
        dz, dc = OFFSETS[k]
        if (dz, dc) == (0, 0):
            g1.append(cp.local(g.at[:, quarter(z * 2 + c)], gg.at[z, c, y]))
            return
        oz, oc = zof(dz), (c + dc) % 2
        g1.append(cp.start(g.at[:, quarter(oz * 2 + oc)], gg.at[z, c, y], device(x, y, oz, oc), gg.at[zof(-dz), oc, y]))

    def wait(copy):
        if copy.is_remote:
            copy.wait_recv()
        else:
            copy.wait()

    up_z, down_z = device(x, y, zof(1), c), device(x, y, zof(-1), c)
    up_y, down_y = device(x, yof(1), z, c), device(x, yof(-1), z, c)
    up_x, down_x = device(xof(1), y, z, c), device(xof(-1), y, z, c)
    sibling = device(x, y, z, (c + 1) % 2)

    h_state = []
    h_sib = {}

    def h_send(pairs, target, back):
        for ref, at, land in pairs:
            back.append(cp.start(ref.at[at], ref.at[at], target, ref.at[land]))

    def h_step(s):
        for copy in h1 if s == 0 else list(h_state):
            wait(copy)
        h_state.clear()
        behind, ahead = zof(-s), zof(s)
        if s < 3:
            h_send([(hg, (behind, c), (zof(-s - 1), c)), (picks, (behind, c), (zof(-s - 1), c))], up_z, h_state)
            h_send([(hg, (ahead, c), (zof(s + 1), c)), (picks, (ahead, c), (zof(s + 1), c))], down_z, h_state)
        elif s == 3:
            low, high = slice(0, 2), slice(2, 4)
            h_send([(hg, (behind, c, low), (zof(-4), c, low)), (picks, (behind, c, low), (zof(-4), c, low))], up_z, h_state)
            h_send([(hg, (ahead, c, high), (zof(4), c, high)), (picks, (ahead, c, high), (zof(4), c, high))], down_z, h_state)
        for d in (-s,) if s in (0, 4) else (-s, s):
            zz = zof(d)
            h_sib[d] = []
            h_send([(r, (zz, c), (zz, (c + 1) % 2)) for r in (hg, picks)], sibling, h_sib[d])

    w_state = {}
    bf16 = jnp.bfloat16
    span = SPAN

    def w_step(s):
        if s == 0:
            for copy in w1:
                wait(copy)

            def widen(i, carry):
                q, r = i // ROWS, i % ROWS
                rows = pl.ds(pl.multiple_of(i * EXPERTS, EXPERTS), EXPERTS)
                for j in range(COLS // 128):
                    wide[j, rows, :] = landed[q, r, :, j * 128 : (j + 1) * 128].astype(jnp.float32)
                return carry

            lax.fori_loop(0, span, widen, 0)

            def turn(e, carry):
                for j in range(COLS // 128):
                    turned[e, :, j * 128 : (j + 1) * 128] = wide[j, pl.ds(e, span, stride=EXPERTS), :].astype(bf16)
                return carry

            lax.fori_loop(0, EXPERTS, turn, 0)
            w_state["up"] = cp.start(turned, wg.at[x], up_x, wg.at[xof(-1)])
            w_state["down"] = cp.start(turned, wg.at[x], down_x, wg.at[xof(1)])
            w_state["own"] = cp.local(turned, wg.at[x])
        else:
            wait(w_state["up"])
            wait(w_state["down"])
            if s == 1:
                low, high = slice(0, EXPERTS // 2), slice(EXPERTS // 2, EXPERTS)
                w_state["up"] = cp.start(wg.at[xof(-1), low], wg.at[xof(-1), low], up_x, wg.at[xof(-2), low])
                w_state["down"] = cp.start(wg.at[xof(1), high], wg.at[xof(1), high], down_x, wg.at[xof(2), high])
            else:
                wait(w_state["own"])

    g2, g3 = [], []
    half = TOK // 2

    def g_first(k):
        wait(g1[k])
        dz, dc = OFFSETS[k]
        zs, cs = zof(-dz), (c + dc) % 2
        mine = gg.at[zs, cs, y]
        g2.append((cp.start(mine, mine, up_y, gg.at[zs, cs, yof(-1)]), cp.start(mine, mine, down_y, gg.at[zs, cs, yof(1)])))

    def g_second(k):
        dz, dc = OFFSETS[k]
        zs, cs = zof(-dz), (c + dc) % 2
        for copy in g2[k]:
            wait(copy)
        below = gg.at[zs, cs, yof(-1), 0:half]
        above = gg.at[zs, cs, yof(1), half:TOK]
        g3.append((
            cp.start(below, below, up_y, gg.at[zs, cs, yof(-2), 0:half]),
            cp.start(above, above, down_y, gg.at[zs, cs, yof(2), half:TOK]),
        ))

    outward = []

    def weigh(k):
        dz, dc = OFFSETS[k]
        zs, cs = zof(-dz), (c + dc) % 2
        for copy in list(g3[k]) + (h_sib[-dz] if dc else []):
            wait(copy)
        outward.append(cp.local(hg.at[zs, cs], hg_out.at[zs, cs]))
        outward.append(cp.local(gg.at[zs, cs], gg_out.at[zs, cs]))

        def one(i, carry):
            at = ((zs * NC + cs) * NY + i) * 2
            which = picks[zs, cs, i]
            mask = jnp.concatenate([which[0:1], which[1:2]], axis=1).astype(jnp.float32).astype(bf16)
            hid, cot = hg[zs, cs, i], gg[zs, cs, i]
            second = hid * mask
            first = hid - second
            total = [
                sums[chain[at + n]] + jnp.dot(part, cot, preferred_element_type=jnp.float32)
                for n, part in enumerate((first, second))
            ]
            for n in range(2):
                sums[at + n] = total[n]
            return carry

        lax.fori_loop(0, NY, one, 0)

    def clear(i, carry):
        sums[i] = jnp.zeros((GROUP, COLS), jnp.float32)
        return carry

    steps = len(OFFSETS)
    for k in range(WINDOW):
        g_start(k)
    h_step(0)
    g_first(0)
    g_first(1)
    lax.fori_loop(0, 2 * NZ * NC * NY + 1, clear, 0)
    weighed = 0
    for k in range(2, steps):
        if k - 2 + WINDOW < steps:
            g_start(k - 2 + WINDOW)
        g_first(k)
        if k == 3:
            w_step(0)
        g_second(k - 2)
        if k in HSTEPS:
            h_step(HSTEPS.index(k) + 1)
        if k == 12:
            w_step(1)
        while weighed < WEIGH[k]:
            weigh(weighed)
            weighed += 1
    g_second(steps - 2)
    g_second(steps - 1)
    while weighed < steps - 2:
        weigh(weighed)
        weighed += 1
    h_step(4)
    for k in range(steps - 2, steps):
        weigh(k)
    outward.append(cp.local(picks, picks_out))

    def settle(e, carry):
        value = sums[chain[2 * NZ * NC * NY + e]]
        for j in range(NX):
            dw[j, e] = value[j * SPAN : (j + 1) * SPAN].astype(bf16)
        return carry

    lax.fori_loop(0, EXPERTS, settle, 0)
    outward.append(cp.local(dw, dw_out))
    w_step(2)
    for copy in outward:
        wait(copy)
    cp.drain()


def add_into(dst, *others):
    lead = dst.shape[:-2]
    rows = dst.shape[-2]
    cut = min(rows, 64)
    per = rows // cut
    total = per
    for n in lead:
        total *= n

    def one(i, carry):
        where, rest = [], i // per
        for n in reversed(lead):
            where.insert(0, rest % n)
            rest = rest // n
        at = tuple(where) + (pl.ds(pl.multiple_of((i % per) * cut, cut), cut), slice(None))
        value = dst[at].astype(jnp.float32)
        for other in others:
            value += other[at].astype(jnp.float32)
        dst[at] = value.astype(jnp.bfloat16)
        return carry

    lax.fori_loop(0, total, one, 0)


def scatter_kernel(slots, w_in, h, g, dw_in, out, hout, wout, w, dw, hv, gv, lo_half_up, lo_half_dn, lo_up, lo_dn, sib, hp_up, hp_dn, dw_half_up, dw_half_dn, dw_up, dw_dn, wide, turned, send, recv):
    x, y, z, c = coords()
    cp = Copies(send, recv)
    zof = lambda d: (z + d + NZ) % NZ
    yof = lambda d: (y + d + NY) % NY
    xof = lambda d: (x + d + NX) % NX
    zl = z % 2
    here = zl * 2 + c
    up_z, down_z = device(x, y, zof(1), c), device(x, y, zof(-1), c)
    up_y, down_y = device(x, yof(1), z, c), device(x, yof(-1), z, c)
    up_x, down_x = device(xof(1), y, z, c), device(xof(-1), y, z, c)
    sibling = device(x, y, z, (c + 1) % 2)
    half = TOK // 2
    low, high = slice(0, EXPERTS // 2), slice(EXPERTS // 2, EXPERTS)
    order = list(reversed(OFFSETS))
    places = [(zof(dz), (c + dc) % 2) for dz, dc in order]

    w_load = cp.local(w_in, w)
    dw_loads = [cp.local(dw_in.at[xof(d)], dw.at[xof(d)]) for d in (2, 1, -1, 0)]
    loads = [(cp.local(h.at[zs, cs], hv.at[zs, cs]), cp.local(g.at[zs, cs], gv.at[zs, cs])) for zs, cs in places]
    greet(x, y, z, c)
    dw_loads[0].wait()
    d_in = (
        cp.start(dw.at[xof(2), low], dw_half_up, up_x, dw_half_up),
        cp.start(dw.at[xof(2), high], dw_half_dn, down_x, dw_half_dn),
    )

    def products(k):
        zs, cs = places[k]
        for copy in loads[k]:
            copy.wait()

        def one(i, carry):
            results = []
            for b in range(TOK // BLOCK):
                slot = slots[((zs * NC + cs) * NY + i) * (TOK // BLOCK) + b]
                weight = jnp.concatenate([w[j, slot] for j in range(NX)], axis=0)
                tokens = slice(b * BLOCK, (b + 1) * BLOCK)
                hid = hv[zs, cs, i, :, tokens]
                cot = gv[zs, cs, i, tokens, :]
                lo = lax.dot_general(hid, weight, (((0,), (0,)), ((), ())), preferred_element_type=jnp.float32)
                hg = lax.dot_general(weight, cot, (((1,), (1,)), ((), ())), preferred_element_type=jnp.float32)
                results.append((tokens, lo, hg))
            for tokens, lo, hg in results:
                gv[zs, cs, i, tokens, :] = lo.astype(jnp.bfloat16)
                hv[zs, cs, i, :, tokens] = hg.astype(jnp.bfloat16)
            return carry

        lax.fori_loop(0, NY, one, 0)

    sib_in, a_in, b_in, o_in = {}, [], [], []

    def lo_first(k):
        zs, cs = places[k]
        a_in.append((
            cp.start(gv.at[zs, cs, yof(2), 0:half], lo_half_up.at[k], up_y, lo_half_up.at[k]),
            cp.start(gv.at[zs, cs, yof(2), half:TOK], lo_half_dn.at[k], down_y, lo_half_dn.at[k]),
        ))
        dz, dc = order[k]
        if dc:
            sib_in[dz] = cp.start(hv.at[zs, cs], sib.at[zs], sibling, sib.at[zs])

    def lo_second(k):
        zs, cs = places[k]
        a_in[k][0].wait_recv()
        add_into(gv.at[zs, cs, yof(1), 0:half], lo_half_up.at[k])
        first = cp.start(gv.at[zs, cs, yof(1)], lo_up.at[k], up_y, lo_up.at[k])
        a_in[k][1].wait_recv()
        add_into(gv.at[zs, cs, yof(-1), half:TOK], lo_half_dn.at[k])
        b_in.append((first, cp.start(gv.at[zs, cs, yof(-1)], lo_dn.at[k], down_y, lo_dn.at[k])))

    def lo_third(k):
        dz, dc = order[k]
        zs, cs = places[k]
        for copy in b_in[k]:
            copy.wait_recv()
        add_into(gv.at[zs, cs, y], lo_up.at[k], lo_dn.at[k])
        mine = out.at[:, quarter(z * 2 + c)]
        if (dz, dc) == (0, 0):
            o_in.append(cp.local(gv.at[zs, cs, y], mine))
        else:
            o_in.append(cp.start(gv.at[zs, cs, y], mine, device(x, y, zs, cs), out.at[:, quarter(zof(-dz) * 2 + cs)]))

    h_state = {}

    def h_step(s):
        for d in (4,) if s == 4 else (s, -s) if s else (0,):
            sib_in[d].wait_recv()
        if s < 4:
            h_state["up"].wait_recv()
            h_state["down"].wait_recv()
        first, last = slice(0, 2), slice(2, 4)
        if s == 4:
            add_into(hv.at[zof(4), c], sib.at[zof(4)])
            h_state["up"] = cp.start(hv.at[zof(4), c, first], hp_up.at[3, first], up_z, hp_up.at[3, first])
            h_state["down"] = cp.start(hv.at[zof(4), c, last], hp_dn.at[3, last], down_z, hp_dn.at[3, last])
            return
        if s == 3:
            add_into(hv.at[zof(3), c, first], sib.at[zof(3), first], hp_up.at[3, first])
            add_into(hv.at[zof(3), c, last], sib.at[zof(3), last])
            add_into(hv.at[zof(-3), c, first], sib.at[zof(-3), first])
            add_into(hv.at[zof(-3), c, last], sib.at[zof(-3), last], hp_dn.at[3, last])
        elif s > 0:
            add_into(hv.at[zof(s), c], sib.at[zof(s)], hp_up.at[s])
            add_into(hv.at[zof(-s), c], sib.at[zof(-s)], hp_dn.at[s])
        else:
            add_into(hv.at[z, c], sib.at[z], hp_up.at[0], hp_dn.at[0])
        if s > 0:
            h_state["up"] = cp.start(hv.at[zof(s), c], hp_up.at[s - 1], up_z, hp_up.at[s - 1])
            h_state["down"] = cp.start(hv.at[zof(-s), c], hp_dn.at[s - 1], down_z, hp_dn.at[s - 1])

    d_state = {}

    def d_step(s):
        if s == 0:
            for copy in dw_loads[1:]:
                copy.wait()
            d_in[0].wait_recv()
            add_into(dw.at[xof(1), low], dw_half_up)
            d_state["up"] = cp.start(dw.at[xof(1)], dw_up, up_x, dw_up)
            d_in[1].wait_recv()
            add_into(dw.at[xof(-1), high], dw_half_dn)
            d_state["down"] = cp.start(dw.at[xof(-1)], dw_dn, down_x, dw_dn)
            return
        d_state["up"].wait_recv()
        d_state["down"].wait_recv()

        def turn(e, carry):
            value = dw[x, e].astype(jnp.float32) + dw_up[e].astype(jnp.float32) + dw_dn[e].astype(jnp.float32)
            for j in range(COLS // 128):
                wide[j, pl.ds(e, SPAN, stride=EXPERTS), :] = value[:, j * 128 : (j + 1) * 128]
            return carry

        lax.fori_loop(0, EXPERTS, turn, 0)

        def narrow(i, carry):
            rows = pl.ds(pl.multiple_of(i * EXPERTS, EXPERTS), EXPERTS)
            for j in range(COLS // 128):
                turned[i // ROWS, i % ROWS, :, j * 128 : (j + 1) * 128] = wide[j, rows, :].astype(jnp.bfloat16)
            return carry

        lax.fori_loop(0, SPAN, narrow, 0)
        for dl, dc in ((1, 0), (1, 1), (0, 1)):
            ol, oc = (zl + dl) % 2, (c + dc) % 2
            there = ol * 2 + oc
            o_in.append(cp.start(turned.at[there], wout.at[:, :, quarter(here)], device(x, y, (z // 2) * 2 + ol, oc), wout.at[:, :, quarter(there)]))
        o_in.append(cp.local(turned.at[here], wout.at[:, :, quarter(here)]))

    steps = len(order)
    w_load.wait()
    for k in range(steps):
        products(k)
        lo_first(k)
        if k >= 1:
            lo_second(k - 1)
        if k >= 3:
            lo_third(k - 3)
        if k in H_BACK:
            h_step(4 - H_BACK.index(k))
        if k == 7:
            d_step(0)
    lo_second(steps - 1)
    lo_third(steps - 3)
    d_step(1)
    lo_third(steps - 2)
    h_step(0)
    for dy in (1, 3, 2):
        oy = yof(dy)
        o_in.append(cp.start(hv.at[z, c, oy], hout.at[y], device(x, oy, z, c), hout.at[yof(-dy)]))
    o_in.append(cp.local(hv.at[z, c, y], hout.at[y]))
    lo_third(steps - 1)
    for copy in o_in:
        if copy.is_remote:
            copy.wait_recv()
        else:
            copy.wait()
    cp.drain()


def body(hidden_rows, out_grad, expert_weights, need_lists, block_pick, owner_slot):
    bf16 = jnp.bfloat16
    shape = jax.ShapeDtypeStruct
    anywhere = pl.BlockSpec(memory_space=pl.ANY)
    ht = hidden_rows.reshape(TOK, NX, 2, NY, NC, ROWS).transpose(3, 1, 2, 4, 5, 0).reshape(NY, GROUP, TOK)
    wt = expert_weights.transpose(1, 0, 2)
    pick = jnp.broadcast_to(jnp.pad(block_pick, (0, 6))[:, None], (8, 128))

    x, y, z, c = coords()
    needs = need_lists.reshape(4, NX, 2, NY, NC, 2)
    needs = lax.dynamic_index_in_dim(needs, x, 1, keepdims=False).transpose(0, 1, 3, 2, 4).reshape(-1)
    ids = jnp.arange(EXPERTS, dtype=jnp.int32)
    known = jnp.sum(jnp.where(needs[:, None] == ids, owner_slot[None, :], 0), axis=1)
    count = known.shape[0]
    place = jnp.arange(count, dtype=jnp.int32)
    far = (z - place // (NC * NY * 2) + NZ) % NZ
    turn = jnp.where(far == 0, 0, jnp.where(far <= NZ // 2, 2 * far - 1, 2 * (NZ - far)))
    rank = (turn * NC + (place // (NY * 2) % NC + c) % NC) * (NY * 2) + place % (NY * 2)
    key = rank * count + place
    before = jnp.max(jnp.where((known[:, None] == known[None, :]) & (key[None, :] < key[:, None]), key[None, :], -1), axis=1)
    final = jnp.max(jnp.where(ids[:, None] == known[None, :], key[None, :], -1), axis=1)
    chain = jnp.concatenate([before, final])
    chain = jnp.where(chain < 0, count, chain % count)

    smem = pl.BlockSpec(memory_space=pltpu.SMEM)
    gathered = (
        shape((NX, EXPERTS, SPAN, COLS), bf16),
        shape((NZ, NC, NY, GROUP, TOK), bf16),
        shape((NZ, NC, NY, TOK, COLS), bf16),
        shape((NZ, NC, NY, 8, 128), jnp.int32),
        shape((NX, EXPERTS, SPAN, COLS), bf16),
    )
    wg, hg, gg, picks, dw = pl.pallas_call(
        gather_kernel,
        out_shape=gathered,
        in_specs=[smem] + [anywhere] * 4,
        out_specs=(anywhere,) * 5,
        scratch_shapes=[
            pltpu.VMEM((NZ, NC, NY, GROUP, TOK), bf16),
            pltpu.VMEM((NZ, NC, NY, TOK, COLS), bf16),
            pltpu.VMEM((NZ, NC, NY, 8, 128), jnp.int32),
            pltpu.VMEM((count + 1, GROUP, COLS), jnp.float32),
            pltpu.VMEM((NX, EXPERTS, SPAN, COLS), bf16),
            pltpu.VMEM((4, ROWS, EXPERTS, COLS), bf16),
            pltpu.VMEM((COLS // 128, SPAN * EXPERTS, 128), jnp.float32),
            pltpu.VMEM((EXPERTS, SPAN, COLS), bf16),
            pltpu.SemaphoreType.DMA((200,)),
            pltpu.SemaphoreType.DMA((200,)),
        ],
        compiler_params=pltpu.CompilerParams(collective_id=0, has_side_effects=True, vmem_limit_bytes=VMEM_LIMIT),
        name="gather",
    )(chain, wt, ht, out_grad, pick)

    known = known.reshape(-1, 2)
    chosen = picks.reshape(-1, 8, 128)[:, 0:2, 0]
    slots = jnp.where(chosen == 0, known[:, 0:1], known[:, 1:2]).reshape(-1)

    half = TOK // 2
    pieces = len(OFFSETS)
    layer_out, hidden, weight_grad = pl.pallas_call(
        scatter_kernel,
        out_shape=(
            shape((TOK, 4096), bf16),
            shape((NY, GROUP, TOK), bf16),
            shape((ROWS, EXPERTS, 1024), bf16),
        ),
        in_specs=[smem] + [anywhere] * 4,
        out_specs=(anywhere,) * 3,
        scratch_shapes=[
            pltpu.VMEM((NX, EXPERTS, SPAN, COLS), bf16),
            pltpu.VMEM((NX, EXPERTS, SPAN, COLS), bf16),
            pltpu.VMEM((NZ, NC, NY, GROUP, TOK), bf16),
            pltpu.VMEM((NZ, NC, NY, TOK, COLS), bf16),
            pltpu.VMEM((pieces, half, COLS), bf16),
            pltpu.VMEM((pieces, half, COLS), bf16),
            pltpu.VMEM((pieces, TOK, COLS), bf16),
            pltpu.VMEM((pieces, TOK, COLS), bf16),
            pltpu.VMEM((NZ, NY, GROUP, TOK), bf16),
            pltpu.VMEM((4, NY, GROUP, TOK), bf16),
            pltpu.VMEM((4, NY, GROUP, TOK), bf16),
            pltpu.VMEM((EXPERTS // 2, SPAN, COLS), bf16),
            pltpu.VMEM((EXPERTS // 2, SPAN, COLS), bf16),
            pltpu.VMEM((EXPERTS, SPAN, COLS), bf16),
            pltpu.VMEM((EXPERTS, SPAN, COLS), bf16),
            pltpu.VMEM((COLS // 128, SPAN * EXPERTS, 128), jnp.float32),
            pltpu.VMEM((4, ROWS, EXPERTS, COLS), bf16),
            pltpu.SemaphoreType.DMA((160,)),
            pltpu.SemaphoreType.DMA((160,)),
        ],
        compiler_params=pltpu.CompilerParams(collective_id=1, has_side_effects=True, vmem_limit_bytes=VMEM_LIMIT),
        name="scatter",
    )(slots, wg, hg, gg, dw)
    hidden_grad = hidden.reshape(NY, NX, 2, NC, ROWS, TOK).transpose(5, 1, 2, 0, 3, 4).reshape(TOK, -1)
    return layer_out, hidden_grad, weight_grad.transpose(1, 0, 2)


def solution(mesh):
    return jax.shard_map(
        body,
        mesh=mesh,
        in_specs=(
            P(("outer", "dev"), None),
            P(("outer", "dev"), None),
            P(None, "dev", "outer"),
            P(),
            P(("outer", "dev")),
            P(),
        ),
        out_specs=(P(("outer", "dev"), None), P(("outer", "dev"), None), P(None, "dev", "outer")),
        check_vma=False,
    )
```

```python
import functools

import jax
import jax.numpy as jnp
from jax import lax
from jax.experimental import pallas as pl
from jax.experimental.pallas import tpu as pltpu
from jax.sharding import PartitionSpec as P

MESH = pl.DeviceIdType.MESH
BLOCK = 128
NX, NY, NZ, NC = 4, 4, 8, 2
ROWS = 12
SPAN = 4 * ROWS
GROUP = 192
COLS = 256
TOK = 256
EXPERTS = 64
VMEM_LIMIT = 60 * 2**20
OFFSETS = [(dz, dc) for dz in (0, 1, -1, 2, -2, 3, -3, 4) for dc in (0, 1)]


WINDOW = 6
HSTEPS = (5, 8, 11)
WEIGH = (0, 0, 0, 0, 1, 2, 3, 4, 5, 6, 7, 8, 9, 10, 11, 12)
H_BACK = (2, 6, 10, 13)
D_BACK = (4, 12)
W_PARTS = (0, 2, 3, 4)
W_STEPS = (6, 14)


def coords():
    o, d = lax.axis_index("outer"), lax.axis_index("dev")
    return d // 16, (d // 2) % 4, o * 2 + (d // 8) % 2, d % 2


def device(x, y, z, c):
    return (z // 2, x * 16 + (z % 2) * 8 + y * 2 + c)


class Copies:
    def __init__(self, send, recv):
        self.send, self.recv, self.used, self.pending = send, recv, 0, []

    def start(self, src, dst, target, land):
        n = self.used
        self.used += 1
        copy = pltpu.make_async_remote_copy(src, dst, self.send.at[n], self.recv.at[n], device_id=target, device_id_type=MESH)
        copy.start()
        self.pending.append(copy)
        back = pltpu.make_async_remote_copy(land, land, self.send.at[n], self.recv.at[n], device_id=target, device_id_type=MESH)
        return back

    def local(self, src, dst):
        n = self.used
        self.used += 1
        copy = pltpu.make_async_copy(src, dst, self.recv.at[n])
        copy.start()
        return copy

    def drain(self):
        for copy in self.pending:
            copy.wait_send()


def greet(x, y, z, c):
    barrier = pltpu.get_barrier_semaphore()
    others = [(x, y, (z + dz + NZ) % NZ, (c + dc) % 2) for dz, dc in OFFSETS[1:]]
    others += [(x, (y + dy) % NY, z, c) for dy in (1, 2, 3)]
    others += [((x + dx) % NX, y, z, c) for dx in (1, 3)]
    for other in others:
        pl.semaphore_signal(barrier, inc=1, device_id=device(*other), device_id_type=MESH)
    return lambda: pl.semaphore_wait(barrier, len(others))


def quarter(q):
    return pl.ds(pl.multiple_of(q * COLS, COLS), COLS)


def gather_kernel(chain, own, w, h, g, wg, hg_out, gg_out, picks_out, dw_out, hg, gg, picks, sums, dw, landed, wide, turned, pick, send, recv):
    x, y, z, c = coords()
    met = greet(x, y, z, c)
    pick[...] = jnp.where(lax.broadcasted_iota(jnp.int32, (8, 128), 0) == 0, own[0], own[1])

    def clear(i, carry):
        sums[i] = jnp.zeros((GROUP, COLS), jnp.float32)
        return carry

    lax.fori_loop(0, 2 * NZ * NC * NY + 1, clear, 0)
    met()
    cp = Copies(send, recv)
    zof = lambda d: (z + d + NZ) % NZ
    yof = lambda d: (y + d + NY) % NY
    xof = lambda d: (x + d + NX) % NX
    zl = z % 2
    here = zl * 2 + c

    h1 = []
    for dy in (1, 3, 2):
        oy = yof(dy)
        h1.append(cp.start(h.at[oy], hg.at[z, c, y], device(x, oy, z, c), hg.at[z, c, yof(-dy)]))
        h1.append(cp.start(pick, picks.at[z, c, y], device(x, oy, z, c), picks.at[z, c, yof(-dy)]))
    h1.append(cp.local(h.at[y], hg.at[z, c, y]))
    h1.append(cp.local(pick, picks.at[z, c, y]))
    w1 = [cp.local(w.at[:, :, quarter(here)], landed.at[here])]

    def w_start(part, parts):
        rows = slice(part * ROWS // parts, (part + 1) * ROWS // parts)
        for dl, dc in ((1, 0), (1, 1), (0, 1)):
            ol, oc = (zl + dl) % 2, (c + dc) % 2
            there = ol * 2 + oc
            w1.append(cp.start(w.at[rows, :, quarter(there)], landed.at[here, rows], device(x, y, (z // 2) * 2 + ol, oc), landed.at[there, rows]))

    g1 = []

    def g_start(k):
        dz, dc = OFFSETS[k]
        if (dz, dc) == (0, 0):
            g1.append(cp.local(g.at[:, quarter(z * 2 + c)], gg.at[z, c, y]))
            return
        oz, oc = zof(dz), (c + dc) % 2
        g1.append(cp.start(g.at[:, quarter(oz * 2 + oc)], gg.at[z, c, y], device(x, y, oz, oc), gg.at[zof(-dz), oc, y]))

    def wait(copy):
        if copy.is_remote:
            copy.wait_recv()
        else:
            copy.wait()

    up_z, down_z = device(x, y, zof(1), c), device(x, y, zof(-1), c)
    up_y, down_y = device(x, yof(1), z, c), device(x, yof(-1), z, c)
    up_x, down_x = device(xof(1), y, z, c), device(xof(-1), y, z, c)
    sibling = device(x, y, z, (c + 1) % 2)

    h_state = []
    h_sib = {}

    def h_send(pairs, target, back):
        for ref, at, land in pairs:
            back.append(cp.start(ref.at[at], ref.at[at], target, ref.at[land]))

    def h_step(s):
        for copy in h1 if s == 0 else list(h_state):
            wait(copy)
        h_state.clear()
        behind, ahead = zof(-s), zof(s)
        if s < 3:
            h_send([(hg, (behind, c), (zof(-s - 1), c)), (picks, (behind, c), (zof(-s - 1), c))], up_z, h_state)
            h_send([(hg, (ahead, c), (zof(s + 1), c)), (picks, (ahead, c), (zof(s + 1), c))], down_z, h_state)
        elif s == 3:
            low, high = slice(0, 2), slice(2, 4)
            h_send([(hg, (behind, c, low), (zof(-4), c, low)), (picks, (behind, c, low), (zof(-4), c, low))], up_z, h_state)
            h_send([(hg, (ahead, c, high), (zof(4), c, high)), (picks, (ahead, c, high), (zof(4), c, high))], down_z, h_state)
        for d in (-s,) if s in (0, 4) else (-s, s):
            zz = zof(d)
            h_sib[d] = []
            h_send([(r, (zz, c), (zz, (c + 1) % 2)) for r in (hg, picks)], sibling, h_sib[d])

    w_state = {}
    bf16 = jnp.bfloat16
    span = SPAN

    def w_step(s):
        if s == 0:
            for copy in w1:
                wait(copy)

            def widen(i, carry):
                q, r = i // ROWS, i % ROWS
                rows = pl.ds(pl.multiple_of(i * EXPERTS, EXPERTS), EXPERTS)
                for j in range(COLS // 128):
                    wide[j, rows, :] = landed[q, r, :, j * 128 : (j + 1) * 128].astype(jnp.float32)
                return carry

            lax.fori_loop(0, span, widen, 0)

            def turn(e, carry):
                for j in range(COLS // 128):
                    turned[e, :, j * 128 : (j + 1) * 128] = wide[j, pl.ds(e, span, stride=EXPERTS), :].astype(bf16)
                return carry

            lax.fori_loop(0, EXPERTS, turn, 0)
            w_state["up"] = cp.start(turned, wg.at[x], up_x, wg.at[xof(-1)])
            w_state["down"] = cp.start(turned, wg.at[x], down_x, wg.at[xof(1)])
            w_state["own"] = cp.local(turned, wg.at[x])
        else:
            wait(w_state["up"])
            wait(w_state["down"])
            if s == 1:
                low, high = slice(0, EXPERTS // 2), slice(EXPERTS // 2, EXPERTS)
                w_state["up"] = cp.start(wg.at[xof(-1), low], wg.at[xof(-1), low], up_x, wg.at[xof(-2), low])
                w_state["down"] = cp.start(wg.at[xof(1), high], wg.at[xof(1), high], down_x, wg.at[xof(2), high])
            else:
                wait(w_state["own"])

    g2, g3 = [], []
    half = TOK // 2

    def g_first(k):
        wait(g1[k])
        dz, dc = OFFSETS[k]
        zs, cs = zof(-dz), (c + dc) % 2
        mine = gg.at[zs, cs, y]
        g2.append((cp.start(mine, mine, up_y, gg.at[zs, cs, yof(-1)]), cp.start(mine, mine, down_y, gg.at[zs, cs, yof(1)])))

    def g_second(k):
        dz, dc = OFFSETS[k]
        zs, cs = zof(-dz), (c + dc) % 2
        for copy in g2[k]:
            wait(copy)
        below = gg.at[zs, cs, yof(-1), 0:half]
        above = gg.at[zs, cs, yof(1), half:TOK]
        g3.append((
            cp.start(below, below, up_y, gg.at[zs, cs, yof(-2), 0:half]),
            cp.start(above, above, down_y, gg.at[zs, cs, yof(2), half:TOK]),
        ))

    outward = []

    def weigh(k):
        dz, dc = OFFSETS[k]
        zs, cs = zof(-dz), (c + dc) % 2
        for copy in list(g3[k]) + (h_sib[-dz] if dc else []):
            wait(copy)
        outward.append(cp.local(hg.at[zs, cs], hg_out.at[zs, cs]))
        outward.append(cp.local(gg.at[zs, cs], gg_out.at[zs, cs]))

        def one(i, carry):
            at = ((zs * NC + cs) * NY + i) * 2
            which = picks[zs, cs, i]
            mask = jnp.concatenate([which[0:1], which[1:2]], axis=1).astype(jnp.float32).astype(bf16)
            hid, cot = hg[zs, cs, i], gg[zs, cs, i]
            second = hid * mask
            first = hid - second
            total = [
                sums[chain[at + n]] + jnp.dot(part, cot, preferred_element_type=jnp.float32)
                for n, part in enumerate((first, second))
            ]
            for n in range(2):
                sums[at + n] = total[n]
            return carry

        lax.fori_loop(0, NY, one, 0)

    steps = len(OFFSETS)
    for part in range(W_PARTS.count(0)):
        w_start(part, len(W_PARTS))
    for k in range(WINDOW):
        g_start(k)
    h_step(0)
    g_first(0)
    g_first(1)
    weighed = 0
    for k in range(2, steps):
        if k - 2 + WINDOW < steps:
            g_start(k - 2 + WINDOW)
        for part in range(len(W_PARTS)):
            if W_PARTS[part] == k:
                w_start(part, len(W_PARTS))
        g_first(k)
        if k == W_STEPS[0]:
            w_step(0)
        g_second(k - 2)
        if k in HSTEPS:
            h_step(HSTEPS.index(k) + 1)
        if k == W_STEPS[1]:
            w_step(1)
        while weighed < WEIGH[k]:
            weigh(weighed)
            weighed += 1
    g_second(steps - 2)
    g_second(steps - 1)
    while weighed < steps - 2:
        weigh(weighed)
        weighed += 1
    h_step(4)
    for k in range(steps - 2, steps):
        weigh(k)
    outward.append(cp.local(picks, picks_out))

    def settle(e, carry):
        value = sums[chain[2 * NZ * NC * NY + e]]
        for j in range(NX):
            dw[j, e] = value[j * SPAN : (j + 1) * SPAN].astype(bf16)
        return carry

    lax.fori_loop(0, EXPERTS, settle, 0)
    outward.append(cp.local(dw, dw_out))
    w_step(2)
    for copy in outward:
        wait(copy)
    cp.drain()


def add_into(dst, *others):
    lead = dst.shape[:-2]
    rows = dst.shape[-2]
    cut = min(rows, 64)
    per = rows // cut
    total = per
    for n in lead:
        total *= n

    def one(i, carry):
        where, rest = [], i // per
        for n in reversed(lead):
            where.insert(0, rest % n)
            rest = rest // n
        at = tuple(where) + (pl.ds(pl.multiple_of((i % per) * cut, cut), cut), slice(None))
        value = dst[at].astype(jnp.float32)
        for other in others:
            value += other[at].astype(jnp.float32)
        dst[at] = value.astype(jnp.bfloat16)
        return carry

    lax.fori_loop(0, total, one, 0)


def scatter_kernel(slots, w_in, h, g, dw_in, out, hout, wout, w, dw, hv, gv, lo_half_up, lo_half_dn, lo_up, lo_dn, sib, hp_up, hp_dn, dw_half_up, dw_half_dn, dw_up, dw_dn, wide, turned, send, recv):
    x, y, z, c = coords()
    cp = Copies(send, recv)
    zof = lambda d: (z + d + NZ) % NZ
    yof = lambda d: (y + d + NY) % NY
    xof = lambda d: (x + d + NX) % NX
    zl = z % 2
    here = zl * 2 + c
    up_z, down_z = device(x, y, zof(1), c), device(x, y, zof(-1), c)
    up_y, down_y = device(x, yof(1), z, c), device(x, yof(-1), z, c)
    up_x, down_x = device(xof(1), y, z, c), device(xof(-1), y, z, c)
    sibling = device(x, y, z, (c + 1) % 2)
    half = TOK // 2
    low, high = slice(0, EXPERTS // 2), slice(EXPERTS // 2, EXPERTS)
    order = list(reversed(OFFSETS))
    places = [(zof(dz), (c + dc) % 2) for dz, dc in order]

    w_load = cp.local(w_in, w)
    dw_loads = [cp.local(dw_in.at[xof(d)], dw.at[xof(d)]) for d in (2, 1, -1, 0)]
    loads = [(cp.local(h.at[zs, cs], hv.at[zs, cs]), cp.local(g.at[zs, cs], gv.at[zs, cs])) for zs, cs in places]
    met = greet(x, y, z, c)

    def start_weights():
        dw_loads[0].wait()
        return (
            cp.start(dw.at[xof(2), low], dw_half_up, up_x, dw_half_up),
            cp.start(dw.at[xof(2), high], dw_half_dn, down_x, dw_half_dn),
        )

    def products(k):
        zs, cs = places[k]
        for copy in loads[k]:
            copy.wait()

        def one(i, carry):
            results = []
            for b in range(TOK // BLOCK):
                slot = slots[((zs * NC + cs) * NY + i) * (TOK // BLOCK) + b]
                weight = jnp.concatenate([w[j, slot] for j in range(NX)], axis=0)
                tokens = slice(b * BLOCK, (b + 1) * BLOCK)
                hid = hv[zs, cs, i, :, tokens]
                cot = gv[zs, cs, i, tokens, :]
                lo = lax.dot_general(hid, weight, (((0,), (0,)), ((), ())), preferred_element_type=jnp.float32)
                hg = lax.dot_general(weight, cot, (((1,), (1,)), ((), ())), preferred_element_type=jnp.float32)
                results.append((tokens, lo, hg))
            for tokens, lo, hg in results:
                gv[zs, cs, i, tokens, :] = lo.astype(jnp.bfloat16)
                hv[zs, cs, i, :, tokens] = hg.astype(jnp.bfloat16)
            return carry

        lax.fori_loop(0, NY, one, 0)

    sib_in, a_in, b_in, o_in = {}, [], [], []

    def lo_first(k):
        zs, cs = places[k]
        a_in.append((
            cp.start(gv.at[zs, cs, yof(2), 0:half], lo_half_up.at[k], up_y, lo_half_up.at[k]),
            cp.start(gv.at[zs, cs, yof(2), half:TOK], lo_half_dn.at[k], down_y, lo_half_dn.at[k]),
        ))
        dz, dc = order[k]
        if dc:
            sib_in[dz] = cp.start(hv.at[zs, cs], sib.at[zs], sibling, sib.at[zs])

    def lo_second(k):
        zs, cs = places[k]
        a_in[k][0].wait_recv()
        add_into(gv.at[zs, cs, yof(1), 0:half], lo_half_up.at[k])
        first = cp.start(gv.at[zs, cs, yof(1)], lo_up.at[k], up_y, lo_up.at[k])
        a_in[k][1].wait_recv()
        add_into(gv.at[zs, cs, yof(-1), half:TOK], lo_half_dn.at[k])
        b_in.append((first, cp.start(gv.at[zs, cs, yof(-1)], lo_dn.at[k], down_y, lo_dn.at[k])))

    def lo_third(k):
        dz, dc = order[k]
        zs, cs = places[k]
        for copy in b_in[k]:
            copy.wait_recv()
        add_into(gv.at[zs, cs, y], lo_up.at[k], lo_dn.at[k])
        mine = out.at[:, quarter(z * 2 + c)]
        if (dz, dc) == (0, 0):
            o_in.append(cp.local(gv.at[zs, cs, y], mine))
        else:
            o_in.append(cp.start(gv.at[zs, cs, y], mine, device(x, y, zs, cs), out.at[:, quarter(zof(-dz) * 2 + cs)]))

    h_state = {}

    def h_step(s):
        for d in (4,) if s == 4 else (s, -s) if s else (0,):
            sib_in[d].wait_recv()
        if s < 4:
            h_state["up"].wait_recv()
            h_state["down"].wait_recv()
        first, last = slice(0, 2), slice(2, 4)
        if s == 4:
            add_into(hv.at[zof(4), c], sib.at[zof(4)])
            h_state["up"] = cp.start(hv.at[zof(4), c, first], hp_up.at[3, first], up_z, hp_up.at[3, first])
            h_state["down"] = cp.start(hv.at[zof(4), c, last], hp_dn.at[3, last], down_z, hp_dn.at[3, last])
            return
        if s == 3:
            add_into(hv.at[zof(3), c, first], sib.at[zof(3), first], hp_up.at[3, first])
            add_into(hv.at[zof(3), c, last], sib.at[zof(3), last])
            add_into(hv.at[zof(-3), c, first], sib.at[zof(-3), first])
            add_into(hv.at[zof(-3), c, last], sib.at[zof(-3), last], hp_dn.at[3, last])
        elif s > 0:
            add_into(hv.at[zof(s), c], sib.at[zof(s)], hp_up.at[s])
            add_into(hv.at[zof(-s), c], sib.at[zof(-s)], hp_dn.at[s])
        else:
            add_into(hv.at[z, c], sib.at[z], hp_up.at[0], hp_dn.at[0])
        if s > 0:
            h_state["up"] = cp.start(hv.at[zof(s), c], hp_up.at[s - 1], up_z, hp_up.at[s - 1])
            h_state["down"] = cp.start(hv.at[zof(-s), c], hp_dn.at[s - 1], down_z, hp_dn.at[s - 1])

    d_state = {}

    def d_step(s):
        if s == 0:
            for copy in dw_loads[1:]:
                copy.wait()
            d_in[0].wait_recv()
            add_into(dw.at[xof(1), low], dw_half_up)
            d_state["up"] = cp.start(dw.at[xof(1)], dw_up, up_x, dw_up)
            d_in[1].wait_recv()
            add_into(dw.at[xof(-1), high], dw_half_dn)
            d_state["down"] = cp.start(dw.at[xof(-1)], dw_dn, down_x, dw_dn)
            return
        d_state["up"].wait_recv()
        d_state["down"].wait_recv()

        def turn(e, carry):
            value = dw[x, e].astype(jnp.float32) + dw_up[e].astype(jnp.float32) + dw_dn[e].astype(jnp.float32)
            for j in range(COLS // 128):
                wide[j, pl.ds(e, SPAN, stride=EXPERTS), :] = value[:, j * 128 : (j + 1) * 128]
            return carry

        lax.fori_loop(0, EXPERTS, turn, 0)

        def narrow(i, carry):
            rows = pl.ds(pl.multiple_of(i * EXPERTS, EXPERTS), EXPERTS)
            for j in range(COLS // 128):
                turned[i // ROWS, i % ROWS, :, j * 128 : (j + 1) * 128] = wide[j, rows, :].astype(jnp.bfloat16)
            return carry

        lax.fori_loop(0, SPAN, narrow, 0)
        for dl, dc in ((1, 0), (1, 1), (0, 1)):
            ol, oc = (zl + dl) % 2, (c + dc) % 2
            there = ol * 2 + oc
            o_in.append(cp.start(turned.at[there], wout.at[:, :, quarter(here)], device(x, y, (z // 2) * 2 + ol, oc), wout.at[:, :, quarter(there)]))
        o_in.append(cp.local(turned.at[here], wout.at[:, :, quarter(here)]))

    steps = len(order)
    w_load.wait()
    products(0)
    met()
    d_in = start_weights()
    for k in range(steps):
        if k > 0:
            products(k)
        lo_first(k)
        if k >= 1:
            lo_second(k - 1)
        if k >= 3:
            lo_third(k - 3)
        if k in H_BACK:
            h_step(4 - H_BACK.index(k))
        if k in D_BACK:
            d_step(D_BACK.index(k))
    lo_second(steps - 1)
    lo_third(steps - 3)
    if len(D_BACK) < 2:
        d_step(1)
    lo_third(steps - 2)
    h_step(0)
    for dy in (1, 3, 2):
        oy = yof(dy)
        o_in.append(cp.start(hv.at[z, c, oy], hout.at[y], device(x, oy, z, c), hout.at[yof(-dy)]))
    o_in.append(cp.local(hv.at[z, c, y], hout.at[y]))
    lo_third(steps - 1)
    for copy in o_in:
        if copy.is_remote:
            copy.wait_recv()
        else:
            copy.wait()
    cp.drain()


def body(hidden_rows, out_grad, expert_weights, need_lists, block_pick, owner_slot):
    bf16 = jnp.bfloat16
    shape = jax.ShapeDtypeStruct
    anywhere = pl.BlockSpec(memory_space=pl.ANY)
    ht = hidden_rows.reshape(TOK, NX, 2, NY, NC, ROWS).transpose(3, 1, 2, 4, 5, 0).reshape(NY, GROUP, TOK)
    wt = expert_weights.transpose(1, 0, 2)

    x, y, z, c = coords()
    needs = need_lists.reshape(4, NX, 2, NY, NC, 2)
    needs = lax.dynamic_index_in_dim(needs, x, 1, keepdims=False).transpose(0, 1, 3, 2, 4).reshape(-1)
    ids = jnp.arange(EXPERTS, dtype=jnp.int32)
    known = jnp.sum(jnp.where(needs[:, None] == ids, owner_slot[None, :], 0), axis=1)
    count = known.shape[0]
    place = jnp.arange(count, dtype=jnp.int32)
    far = (z - place // (NC * NY * 2) + NZ) % NZ
    turn = jnp.where(far == 0, 0, jnp.where(far <= NZ // 2, 2 * far - 1, 2 * (NZ - far)))
    rank = (turn * NC + (place // (NY * 2) % NC + c) % NC) * (NY * 2) + place % (NY * 2)
    key = rank * count + place
    before = jnp.max(jnp.where((known[:, None] == known[None, :]) & (key[None, :] < key[:, None]), key[None, :], -1), axis=1)
    final = jnp.max(jnp.where(ids[:, None] == known[None, :], key[None, :], -1), axis=1)
    chain = jnp.concatenate([before, final])
    chain = jnp.where(chain < 0, count, chain % count)

    smem = pl.BlockSpec(memory_space=pltpu.SMEM)
    gathered = (
        shape((NX, EXPERTS, SPAN, COLS), bf16),
        shape((NZ, NC, NY, GROUP, TOK), bf16),
        shape((NZ, NC, NY, TOK, COLS), bf16),
        shape((NZ, NC, NY, 8, 128), jnp.int32),
        shape((NX, EXPERTS, SPAN, COLS), bf16),
    )
    wg, hg, gg, picks, dw = pl.pallas_call(
        gather_kernel,
        out_shape=gathered,
        in_specs=[smem] * 2 + [anywhere] * 3,
        out_specs=(anywhere,) * 5,
        scratch_shapes=[
            pltpu.VMEM((NZ, NC, NY, GROUP, TOK), bf16),
            pltpu.VMEM((NZ, NC, NY, TOK, COLS), bf16),
            pltpu.VMEM((NZ, NC, NY, 8, 128), jnp.int32),
            pltpu.VMEM((count + 1, GROUP, COLS), jnp.float32),
            pltpu.VMEM((NX, EXPERTS, SPAN, COLS), bf16),
            pltpu.VMEM((4, ROWS, EXPERTS, COLS), bf16),
            pltpu.VMEM((COLS // 128, SPAN * EXPERTS, 128), jnp.float32),
            pltpu.VMEM((EXPERTS, SPAN, COLS), bf16),
            pltpu.VMEM((8, 128), jnp.int32),
            pltpu.SemaphoreType.DMA((200,)),
            pltpu.SemaphoreType.DMA((200,)),
        ],
        compiler_params=pltpu.CompilerParams(collective_id=0, has_side_effects=True, vmem_limit_bytes=VMEM_LIMIT),
        name="gather",
    )(chain, block_pick, wt, ht, out_grad)

    known = known.reshape(-1, 2)
    chosen = picks.reshape(-1, 8, 128)[:, 0:2, 0]
    slots = jnp.where(chosen == 0, known[:, 0:1], known[:, 1:2]).reshape(-1)

    half = TOK // 2
    pieces = len(OFFSETS)
    layer_out, hidden, weight_grad = pl.pallas_call(
        scatter_kernel,
        out_shape=(
            shape((TOK, 4096), bf16),
            shape((NY, GROUP, TOK), bf16),
            shape((ROWS, EXPERTS, 1024), bf16),
        ),
        in_specs=[smem] + [anywhere] * 4,
        out_specs=(anywhere,) * 3,
        scratch_shapes=[
            pltpu.VMEM((NX, EXPERTS, SPAN, COLS), bf16),
            pltpu.VMEM((NX, EXPERTS, SPAN, COLS), bf16),
            pltpu.VMEM((NZ, NC, NY, GROUP, TOK), bf16),
            pltpu.VMEM((NZ, NC, NY, TOK, COLS), bf16),
            pltpu.VMEM((pieces, half, COLS), bf16),
            pltpu.VMEM((pieces, half, COLS), bf16),
            pltpu.VMEM((pieces, TOK, COLS), bf16),
            pltpu.VMEM((pieces, TOK, COLS), bf16),
            pltpu.VMEM((NZ, NY, GROUP, TOK), bf16),
            pltpu.VMEM((4, NY, GROUP, TOK), bf16),
            pltpu.VMEM((4, NY, GROUP, TOK), bf16),
            pltpu.VMEM((EXPERTS // 2, SPAN, COLS), bf16),
            pltpu.VMEM((EXPERTS // 2, SPAN, COLS), bf16),
            pltpu.VMEM((EXPERTS, SPAN, COLS), bf16),
            pltpu.VMEM((EXPERTS, SPAN, COLS), bf16),
            pltpu.VMEM((COLS // 128, SPAN * EXPERTS, 128), jnp.float32),
            pltpu.VMEM((4, ROWS, EXPERTS, COLS), bf16),
            pltpu.SemaphoreType.DMA((160,)),
            pltpu.SemaphoreType.DMA((160,)),
        ],
        compiler_params=pltpu.CompilerParams(collective_id=1, has_side_effects=True, vmem_limit_bytes=VMEM_LIMIT),
        name="scatter",
    )(slots, wg, hg, gg, dw)
    hidden_grad = hidden.reshape(NY, NX, 2, NC, ROWS, TOK).transpose(5, 1, 2, 0, 3, 4).reshape(TOK, -1)
    return layer_out, hidden_grad, weight_grad.transpose(1, 0, 2)


def solution(mesh):
    return jax.shard_map(
        body,
        mesh=mesh,
        in_specs=(
            P(("outer", "dev"), None),
            P(("outer", "dev"), None),
            P(None, "dev", "outer"),
            P(),
            P(("outer", "dev")),
            P(),
        ),
        out_specs=(P(("outer", "dev"), None), P(("outer", "dev"), None), P(None, "dev", "outer")),
        check_vma=False,
    )
```
